128 devices in a mesh: gx: 8 (over z, core), gy: 16 (over y, x).
Axes of the slice: x: 4, y: 4, z: 4, core: 2. Of those that a mesh axis runs over, the one named last changes fastest.
Arguments:
- token_ids: int32 [8, 64], replicated, may hold values from 0 to 65535
- cache_lengths: int32 [64], P('gy'), may hold values from 512 to 8192, as said below
- embed_table: bfloat16 [65536, 8192], P('gx', 'gy'), may hold values from -120 to 120
- norm_gain: bfloat16 [8192], P('gy'), may hold values from 0.099609375 to 1.8984375
- qkv_weight: bfloat16 [8192, 10240], P('gy', 'gx'), may hold values from -0.0625 to 0.0625
- key_cache: bfloat16 [64, 8192, 1024], P('gy', None, 'gx'), may hold values from -80 to 80
- value_cache: bfloat16 [64, 8192, 1024], P('gy', None, 'gx'), may hold values from -6 to 6
- out_weight: bfloat16 [8192, 8192], P('gx', 'gy'), may hold values from -0.5 to 0.5
Outputs:
- attn_out: bfloat16 [8, 64, 8192], P(None, 'gx', 'gy')
- new_kv: bfloat16 [2, 8, 64, 1024], P(None, None, 'gy', 'gx')
The draws below stay inside these ranges and needn't reach their ends.
Inputs may be any that keep to these rules, and one draw needn't show every extreme that they name: `cache_lengths`: at least 512; one row of every draw holds exactly 8192.
All inputs are finite; a program needn't handle non-finite values.
Results may differ from the reference program's by a relative error of at most 0.012.
Values may be sent and summed in bfloat16 or wider, within the bound.
A program may use at most 128 MiB of HBM per device.

```python
import math
import jax
import jax.numpy as jnp
from jax import lax

D = 8192
HQ = 64
KVH = 8
HD = 128
VOCAB = 65536
CTX = 8192
STEPS = 8
GROUP = 8
ROWS = 64


def draw_cache_lengths(key, part):
    key = jax.random.fold_in(key, 5)
    first_key, second_key = jax.random.split(key)
    lengths = jax.random.randint(first_key, (ROWS,), CTX // 16, CTX + 1)
    chosen = jax.random.randint(second_key, (), 0, ROWS)
    return jnp.where(jnp.arange(ROWS) == chosen, CTX, lengths).astype(jnp.int32)


def draw_embed_table(key, part):
    key = jax.random.fold_in(key, 7)
    entry_key, row_key, column_key = jax.random.split(key, 3)
    columns = jnp.arange(D, dtype=jnp.float32) / D
    rough = jnp.exp(jax.random.uniform(column_key, (1, D), jnp.float32, -0.35, 0.35))
    entries = jnp.clip(jax.random.normal(entry_key, (VOCAB, D), jnp.float32), -6.0, 6.0)
    row_scale = jnp.exp(jax.random.uniform(row_key, (VOCAB, 1), jnp.float32, math.log(0.3), math.log(3.0)))
    ramp = jnp.power(3.0, columns)[None, :]
    return (entries * row_scale * ramp * rough).astype(jnp.bfloat16)


def draw_key_cache(key, part):
    key = jax.random.fold_in(key, 11)
    base_key = jax.random.fold_in(key, 0)
    shape = (ROWS, CTX, KVH * HD)
    return jnp.clip(jax.random.normal(base_key, shape, jnp.float32) * 1.5, -7.5, 7.5).astype(jnp.bfloat16)


def place_ends(values, key, low, high):
    spot = [jax.random.randint(jax.random.fold_in(key, axis), (), 0, length) for axis, length in enumerate(values.shape)]
    main_axis = values.shape.index(max(values.shape))
    neighbour = spot[:main_axis] + [(spot[main_axis] + 1) % values.shape[main_axis]] + spot[main_axis + 1:]
    return values.at[tuple(spot)].set(low).at[tuple(neighbour)].set(high)


def shard_levels(own_key, dims, cuts, smallest, high):
    gain = 1.0
    for axis_at, parts in cuts:
        heights = jax.random.uniform(jax.random.fold_in(jax.random.fold_in(own_key, 6), axis_at), (parts,), jnp.float32, smallest / len(cuts), high / len(cuts))
        gain = gain * jnp.repeat(jnp.exp(heights), dims[axis_at] // parts).reshape((-1,) + (1,) * (len(dims) - 1 - axis_at))
    return gain


def normal_values(own_key, shape, width, reach, pieces=(), kind=jnp.bfloat16):
    result = jax.random.normal(own_key, shape, jnp.float32) * width
    if len(pieces) > 0:
        result = shard_levels(own_key, shape, pieces, -0.22, 0.18) * result
    return jnp.clip(result, min=-reach, max=reach).astype(kind)


def setup_inputs(seed: int = 0) -> dict:
    key_list = jax.random.split(jax.random.key(seed), 9)
    return {
        "token_ids": place_ends(jax.random.randint(key_list[0], (STEPS, ROWS), 0, VOCAB), jax.random.fold_in(key_list[0], 1), 0, VOCAB - 1).astype(jnp.int32),
        "cache_lengths": draw_cache_lengths(jax.random.fold_in(key_list[8], 71), 0),
        "embed_table": draw_embed_table(jax.random.fold_in(key_list[8], 71), 0),
        "norm_gain": jnp.clip(1.0 + 0.18 * jax.random.normal(key_list[3], (D,), jnp.float32), 0.099609375, 1.8984375).astype(jnp.bfloat16),
        "qkv_weight": normal_values(key_list[4], (D, KVH * (GROUP + 2) * HD), D ** -0.5, 0.0625, ((0, 16), (1, 8))),
        "key_cache": draw_key_cache(jax.random.fold_in(key_list[8], 71), 0),
        "value_cache": normal_values(key_list[6], (ROWS, CTX, KVH * HD), 1.0, 6.0, ((0, 16), (2, 8))),
        "out_weight": normal_values(key_list[7], (HQ * HD, D), HD ** -0.5, 0.5, ((0, 8), (1, 16))),
    }


THETA = 500000.0
EPS = 1e-05
MASKED = -1e+30

def rotate(field, positions):
    half_width = field.shape[-1] // 2
    inverse_freq = jnp.power(jnp.float32(THETA), -jnp.arange(half_width, dtype=jnp.float32) * (2.0 / field.shape[-1]))
    angles = positions[..., None].astype(jnp.float32) * inverse_freq
    front_half = field[..., :half_width]
    back_half = field[..., half_width:]
    cosine = jnp.cos(angles)
    sine = jnp.sin(angles)
    return jnp.concatenate([front_half * cosine - back_half * sine, back_half * cosine + front_half * sine], -1)

def reference(token_ids, cache_lengths, embed_table, norm_gain, qkv_weight, key_cache, value_cache, out_weight):
    embedded = embed_table[token_ids].astype(jnp.float32)
    inverse_rms = lax.rsqrt(lax.optimization_barrier(jnp.mean(embedded * embedded, -1)) + EPS)
    scaled = (embedded * norm_gain.astype(jnp.float32)).astype(jnp.bfloat16)
    projected = jnp.dot(scaled.reshape(STEPS * ROWS, D), qkv_weight, preferred_element_type=jnp.float32)
    projected = projected * inverse_rms.reshape(STEPS * ROWS, 1)
    projected = projected.reshape(STEPS, ROWS, KVH, GROUP + 2, HD)
    positions = cache_lengths[None, :] + jnp.arange(STEPS, dtype=jnp.int32)[:, None]
    queries = (rotate(projected[:, :, :, :GROUP], positions[:, :, None, None]) * HD ** (-0.5)).astype(jnp.bfloat16)
    fresh_keys = rotate(projected[:, :, :, GROUP], positions[:, :, None]).astype(jnp.bfloat16)
    fresh_values = projected[:, :, :, GROUP + 1].astype(jnp.bfloat16)
    valid = jnp.arange(CTX, dtype=jnp.int32)[None, :] < cache_lengths[:, None]
    allowed = jnp.arange(STEPS, dtype=jnp.int32)[None, :] <= jnp.arange(STEPS, dtype=jnp.int32)[:, None]

    def one_head(head):
        cache_k = lax.dynamic_slice_in_dim(key_cache, head * HD, HD, 2).astype(jnp.float32)
        cache_v = lax.dynamic_slice_in_dim(value_cache, head * HD, HD, 2).astype(jnp.float32)
        head_q = lax.dynamic_index_in_dim(queries, head, 2, keepdims=False).astype(jnp.float32)
        new_k = lax.dynamic_index_in_dim(fresh_keys, head, 2, keepdims=False).astype(jnp.float32)
        new_v = lax.dynamic_index_in_dim(fresh_values, head, 2, keepdims=False).astype(jnp.float32)
        cache_scores = jnp.einsum('srgd,rpd->srgp', head_q, cache_k, precision=lax.Precision.HIGHEST)
        cache_scores = jnp.where(valid[None, :, None, :], cache_scores, MASKED)
        fresh_scores = jnp.einsum('srgd,urd->srgu', head_q, new_k, precision=lax.Precision.HIGHEST)
        fresh_scores = jnp.where(allowed[:, None, None, :], fresh_scores, MASKED)
        largest = jnp.maximum(lax.optimization_barrier(jnp.max(cache_scores, -1)), lax.optimization_barrier(jnp.max(fresh_scores, -1)))[..., None]
        cache_exp = jnp.exp(cache_scores - largest)
        fresh_exp = jnp.exp(fresh_scores - largest)
        denominator = (lax.optimization_barrier(jnp.sum(cache_exp, -1)) + lax.optimization_barrier(jnp.sum(fresh_exp, -1)))[..., None]
        cache_weights = (cache_exp / denominator).astype(jnp.bfloat16).astype(jnp.float32)
        fresh_weights = (fresh_exp / denominator).astype(jnp.bfloat16).astype(jnp.float32)
        attended = jnp.einsum('srgp,rpd->srgd', cache_weights, cache_v, precision=lax.Precision.HIGHEST)
        attended = attended + jnp.einsum('srgu,urd->srgd', fresh_weights, new_v, precision=lax.Precision.HIGHEST)
        return attended.astype(jnp.bfloat16)
    per_head = lax.map(one_head, jnp.arange(KVH, dtype=jnp.int32))
    attended = jnp.transpose(per_head, (1, 2, 0, 3, 4)).reshape(STEPS * ROWS, HQ * HD)
    attn_out = jnp.dot(attended, out_weight, preferred_element_type=jnp.float32).reshape(STEPS, ROWS, D).astype(jnp.bfloat16)
    new_kv = jnp.stack([fresh_keys.reshape(STEPS, ROWS, KVH * HD), fresh_values.reshape(STEPS, ROWS, KVH * HD)])
    return (attn_out, new_kv)
```

```python
import functools
import math

import jax
import jax.numpy as jnp
import numpy as np
from jax import lax
from jax.experimental import pallas as pl
from jax.experimental.pallas import tpu as pltpu
from jax.sharding import PartitionSpec as P

D = 8192
HD = 128
GROUP = 8
STEPS = 8
THETA = 500000.0
EPS = 1e-05
MASKED = -1e30
MESH = pl.DeviceIdType.MESH

NCH = 2
RPC = 2
TPD = RPC * STEPS
TOK = 16 * TPD
SL = TOK // 8
TBLK = 1024
PBLK = 1024
F32 = jnp.float32
BF16 = jnp.bfloat16


def iota(shape, dim):
    return lax.broadcasted_iota(jnp.int32, shape, dim)


def kernel(
    ids_ref, len_ref, gain_ref, freq_ref, table_hbm, wqkv_hbm, key_hbm, val_hbm, wout_hbm,
    out_ref, kv_ref,
    table, wqkv, wout, kbuf, vbuf, acc,
    picks, r1a, s1, r1b, eall, part, ra, sb, rb, sq, rsq, ag, part5, r5a, s5, r5b, fin, kvs,
    local_sem, table_sem, send_sem, recv_sem,
):
    gx = lax.axis_index("gx")
    gy = lax.axis_index("gy")
    z, core = gx // 2, gx % 2
    y, x = gy // 4, gy % 4

    def wrap(a, k):
        return (a + k) % 4

    def at_core():
        return (z * 2 + 1 - core, gy)

    def at_z(k):
        return (wrap(z, k) * 2 + core, gy)

    def at_y(k):
        return (gx, wrap(y, k) * 4 + x)

    def at_x(k):
        return (gx, y * 4 + wrap(x, k))

    counter = [0]
    sends = []

    def remote(src, dst, device):
        n = counter[0]
        counter[0] += 1
        copy = pltpu.make_async_remote_copy(
            src_ref=src, dst_ref=dst, send_sem=send_sem.at[n], recv_sem=recv_sem.at[n],
            device_id=device, device_id_type=MESH,
        )
        copy.start()
        sends.append(copy)
        return copy

    nblk = table.shape[0]
    table_copies = []
    for b in range(nblk):
        copy = pltpu.make_async_copy(
            table_hbm.at[pl.ds(b * TBLK, TBLK)], table.at[b], table_sem.at[b]
        )
        copy.start()
        table_copies.append(copy)
    load_w = pltpu.make_async_copy(wqkv_hbm, wqkv, local_sem.at[0])
    load_o = pltpu.make_async_copy(wout_hbm, wout, local_sem.at[1])
    load_w.start()
    load_kv = []
    for c in range(NCH):
        rows = pl.ds(c * RPC, RPC)
        load_kv.append((
            pltpu.make_async_copy(key_hbm.at[rows], kbuf.at[rows], local_sem.at[2 + 2 * c]),
            pltpu.make_async_copy(val_hbm.at[rows], vbuf.at[rows], local_sem.at[3 + 2 * c]),
        ))
        for copy in load_kv[c]:
            copy.start()
    load_o.start()

    barrier = pltpu.get_barrier_semaphore()
    partners = [at_core()]
    for k in (1, 2, 3):
        partners += [at_z(k), at_y(k), at_x(k)]
    for device in partners:
        pl.semaphore_signal(barrier, inc=1, device_id=device, device_id_type=MESH)

    ids = ids_ref[...]
    id_high = (ids >> 8).astype(F32).astype(BF16)
    id_low = (ids & 255).astype(F32).astype(BF16)

    def local_ids(c):
        token = iota((TOK, 64), 0)
        row = (token // TPD) * (NCH * RPC) + c * RPC + (token // STEPS) % RPC
        chosen = jnp.where(iota((TOK, 64), 1) == row, 1.0, 0.0).astype(BF16)
        contract = (((1,), (1,)), ((), ()))
        high = lax.dot_general(chosen, id_high, contract, preferred_element_type=F32)
        low = lax.dot_general(chosen, id_low, contract, preferred_element_type=F32)
        both = high * 256.0 + low
        mine = iota((TOK, STEPS), 1) == iota((TOK, STEPS), 0) % STEPS
        column = jnp.sum(jnp.where(mine, both, 0.0), axis=1, keepdims=True)
        return column.astype(jnp.int32) - gx * (nblk * TBLK)

    def gather(c, first):
        local = local_ids(c)
        for b in range(nblk):
            if first:
                table_copies[b].wait()
            hot = jnp.where(iota((TOK, TBLK), 1) == local - b * TBLK, 1.0, 0.0).astype(BF16)
            term = jnp.dot(hot, table[b], preferred_element_type=F32)
            if b == 0:
                acc[...] = term
            else:
                acc[...] += term
        picks[c] = acc[...].astype(BF16).reshape(picks.shape[1:])

    def send_1a(c):
        return remote(picks.at[c, :, 1 - core], r1a.at[c], at_core())

    def send_1b(c, copy):
        copy.wait_recv()
        s1[c] = picks[c, :, core] + r1a[c]
        return [remote(s1.at[c, wrap(z, k)], r1b.at[c, k - 1], at_z(k)) for k in (1, 2, 3)]

    def send_1c(c, copies):
        for copy in copies:
            copy.wait_recv()
        eall[c, z, core] = (s1[c, z] + r1b[c, 0]) + (r1b[c, 1] + r1b[c, 2])
        mine = eall.at[c, z, core]
        return (
            [remote(mine, mine, at_z(k)) for k in (1, 2, 3)],
            [remote(mine, mine, at_core())],
        )

    def send_1d(c, copies):
        across, over = copies
        for k, copy in zip((1, 2, 3), across):
            copy.wait_recv()
            block = eall.at[c, wrap(z, 4 - k), core]
            over.append(remote(block, block, at_core()))
        return over

    half = wqkv.shape[1] // 2

    def send_2a(c, copies):
        for copy in copies:
            copy.wait_recv()
        embedded = eall[c].reshape(TOK, eall.shape[-1]).astype(F32)
        scaled = (embedded * gain_ref[...].astype(F32)).astype(BF16)
        product = jnp.dot(scaled, wqkv[...], preferred_element_type=F32)
        part[c] = product.astype(BF16).reshape(part.shape[1:])
        out = []
        for k in (1, 2, 3):
            out.append(remote(
                part.at[c, :, wrap(x, k), :, pl.ds(0, half)], ra.at[c, 0, k - 1], at_x(k)
            ))
            out.append(remote(
                part.at[c, wrap(y, k), :, :, pl.ds(half, half)], ra.at[c, 1, k - 1], at_y(k)
            ))
        squares = embedded * embedded
        high = squares.astype(BF16)
        low = (squares - high.astype(F32)).astype(BF16)
        ones = jnp.ones((8, eall.shape[-1]), BF16)
        contract = (((1,), (1,)), ((), ()))
        total = lax.dot_general(ones, high, contract, preferred_element_type=F32)
        total = total + lax.dot_general(ones, low, contract, preferred_element_type=F32)
        sq[c, 0] = total[:1]
        for k in (1, 2, 3):
            out.append(remote(sq.at[c, 0], rsq.at[c, 0, k - 1], at_x(k)))
        return out

    def send_2b(c, copies):
        for copy in copies:
            copy.wait_recv()
        sq[c, 1] = (sq[c, 0] + rsq[c, 0, 0]) + (rsq[c, 0, 1] + rsq[c, 0, 2])
        out = []
        for h, own in ((0, part[c, :, x, :, pl.ds(0, half)]), (1, part[c, y, :, :, pl.ds(half, half)])):
            total = own.astype(F32)
            for k in range(3):
                total = total + ra[c, h, k].astype(F32)
            sb[c, h] = total.astype(BF16)
        for k in (1, 2, 3):
            out.append(remote(sb.at[c, 0, wrap(y, k)], rb.at[c, 0, k - 1], at_y(k)))
            out.append(remote(sb.at[c, 1, wrap(x, k)], rb.at[c, 1, k - 1], at_x(k)))
            out.append(remote(sq.at[c, 1], rsq.at[c, 1, k - 1], at_y(k)))
        return out

    def queries(c, copies):
        for copy in copies:
            copy.wait_recv()
        squares = (sq[c, 1] + rsq[c, 1, 0]) + (rsq[c, 1, 1] + rsq[c, 1, 2])
        place = iota((TPD, TOK), 1) == iota((TPD, TOK), 0) + gy * TPD
        column = jnp.sum(jnp.where(place, squares, 0.0), axis=1, keepdims=True)
        inverse_rms = lax.rsqrt(column / D + EPS)
        pieces = []
        for h, own in ((0, sb[c, 0, y]), (1, sb[c, 1, x])):
            total = own.astype(F32)
            for k in range(3):
                total = total + rb[c, h, k].astype(F32)
            pieces.append(total)
        projected = jnp.concatenate(pieces, axis=1) * inverse_rms
        sub = iota((TPD, 1), 0)
        length = jnp.where(sub < STEPS, len_ref[c * RPC], len_ref[c * RPC + 1])
        position = (length + sub % STEPS).astype(F32)
        angle = position * freq_ref[...]
        cosine = jnp.cos(angle)
        sine = jnp.sin(angle)
        sine = jnp.where(iota((TPD, HD), 1) < HD // 2, -sine, sine)

        def rotate(g):
            field = projected[:, g * HD : (g + 1) * HD]
            return field * cosine + pltpu.roll(field, HD // 2, 1) * sine

        heads = [rotate(g) * HD ** (-0.5) for g in range(GROUP)]
        new_key = rotate(GROUP).astype(BF16)
        new_value = projected[:, (GROUP + 1) * HD :].astype(BF16)
        kvs[pl.ds(c * TPD, TPD)] = jnp.concatenate([new_key, new_value], axis=1)
        rows = [
            jnp.concatenate([head[r * STEPS : (r + 1) * STEPS] for head in heads], axis=0)
            for r in range(RPC)
        ]
        return rows, new_key, new_value

    nq = GROUP * STEPS

    def attention_start(rows, new_key, new_value):
        plain = jnp.concatenate(rows, axis=0).astype(BF16)
        nothing = jnp.zeros_like(rows[0])
        paired = jnp.concatenate(
            [
                jnp.concatenate([rows[0], nothing], axis=1),
                jnp.concatenate([nothing, rows[1]], axis=1),
            ],
            axis=0,
        ).astype(BF16)
        scores = lax.dot_general(
            plain, new_key, (((1,), (1,)), ((), ())), preferred_element_type=F32
        )
        query = iota(scores.shape, 0)
        entry = iota(scores.shape, 1)
        allowed = (entry // STEPS == query // nq) & (entry % STEPS <= query % STEPS)
        scores = jnp.where(allowed, scores, MASKED)
        largest = jnp.max(scores, axis=1, keepdims=True)
        weights = jnp.where(allowed, jnp.exp(scores - largest), 0.0)
        total = jnp.sum(weights, axis=1, keepdims=True)
        value = jnp.dot(weights.astype(BF16), new_value, preferred_element_type=F32)
        return paired, (largest, total, jnp.concatenate([value, value], axis=1))

    def attention_blocks(c, paired, state, first, last):
        r = c * RPC
        limits = (len_ref[r], len_ref[r + 1])

        def step(b, state):
            largest, total, value = state
            start = pl.multiple_of(b * PBLK, PBLK)
            where = pl.ds(start, PBLK)
            keys = jnp.concatenate([kbuf[r, where], kbuf[r + 1, where]], axis=1)
            values = jnp.concatenate([vbuf[r, where], vbuf[r + 1, where]], axis=1)
            scores = lax.dot_general(
                paired, keys, (((1,), (1,)), ((), ())), preferred_element_type=F32
            )
            place = iota((nq, PBLK), 1) + start
            scores = jnp.concatenate(
                [
                    jnp.where(place < limits[0], scores[:nq], MASKED),
                    jnp.where(place < limits[1], scores[nq:], MASKED),
                ],
                axis=0,
            )
            larger = jnp.maximum(largest, jnp.max(scores, axis=1, keepdims=True))
            shrink = jnp.exp(largest - larger)
            weights = jnp.exp(scores - larger)
            total = total * shrink + jnp.sum(weights, axis=1, keepdims=True)
            value = value * shrink + jnp.dot(
                weights.astype(BF16), values, preferred_element_type=F32
            )
            return larger, total, value

        return lax.fori_loop(first, last, step, state)

    def send_4a(c, state):
        _, total, value = state
        value = value / total
        columns = []
        for g in range(GROUP):
            columns.append(jnp.concatenate(
                [
                    value[r * nq + g * STEPS : r * nq + (g + 1) * STEPS, r * HD : (r + 1) * HD]
                    for r in range(RPC)
                ],
                axis=0,
            ))
        ag[c, 0, 0] = jnp.concatenate(columns, axis=1).astype(BF16)
        own = ag.at[c, 0, 0]
        out = ([], [])
        for k in (1, 2, 3):
            out[0].append(remote(own, ag.at[c, 0, k], at_x(k)))
            out[1].append(remote(own, ag.at[c, k, 0], at_y(k)))
        return out

    ahalf = wout.shape[0] // 2

    def send_4b(c, copies):
        along_x, along_y = copies
        out = []
        left, right = pl.ds(0, ahalf), pl.ds(ahalf, ahalf)
        others = pl.ds(1, 3)
        for copy in along_x:
            copy.wait_recv()
        for k in (1, 2, 3):
            out.append(remote(
                ag.at[c, 0, others, :, left], ag.at[c, k, others, :, left], at_y(k)
            ))
        for copy in along_y:
            copy.wait_recv()
        for k in (1, 2, 3):
            out.append(remote(
                ag.at[c, others, 0, :, right], ag.at[c, others, k, :, right], at_x(k)
            ))
        return out

    def send_5a(c, copies):
        for copy in copies:
            copy.wait_recv()
        everyone = ag[c].reshape(TOK, wout.shape[0])
        product = jnp.dot(everyone, wout[...], preferred_element_type=F32).astype(BF16)
        for ky in range(4):
            for kx in range(4):
                n = (ky * 4 + kx) * TPD
                place = wrap(x, 4 - kx)
                part5[c, wrap(y, 4 - ky), place // 2, place % 2] = product[n : n + TPD]
        return remote(part5.at[c, :, 1 - core], r5a.at[c], at_core())

    def send_5b(c, copy):
        copy.wait_recv()
        s5[c] = (part5[c, :, core].astype(F32) + r5a[c].astype(F32)).astype(BF16)
        return [remote(s5.at[c, wrap(z, k)], r5b.at[c, k - 1], at_z(k)) for k in (1, 2, 3)]

    def finish(c, copies):
        for copy in copies:
            copy.wait_recv()
        total = s5[c, z].astype(F32)
        for k in range(3):
            total = total + r5b[c, k].astype(F32)
        fin[pl.ds(c * SL, SL)] = total.astype(BF16).reshape(SL, total.shape[-1])

    gather(0, True)
    pl.semaphore_wait(barrier, len(partners))
    a1 = send_1a(0)
    gather(1, False)
    b1 = send_1a(1)
    a1 = send_1b(0, a1)
    b1 = send_1b(1, b1)
    a1 = send_1c(0, a1)
    b1 = send_1c(1, b1)
    a1 = send_1d(0, a1)
    load_w.wait()
    b1 = send_1d(1, b1)
    a2 = send_2a(0, a1)
    b2 = send_2a(1, b1)
    a2 = send_2b(0, a2)
    b2 = send_2b(1, b2)
    nb = kbuf.shape[1] // PBLK
    a_rows, a_key, a_value = queries(0, a2)
    for copy in load_kv[0]:
        copy.wait()
    paired, state = attention_start(a_rows, a_key, a_value)
    state = attention_blocks(0, paired, state, 0, nb)
    a4 = send_4a(0, state)
    b_rows, b_key, b_value = queries(1, b2)
    for copy in load_kv[1]:
        copy.wait()
    paired, state = attention_start(b_rows, b_key, b_value)
    state = attention_blocks(1, paired, state, 0, nb)
    b4 = send_4a(1, state)
    a4 = send_4b(0, a4)
    b4 = send_4b(1, b4)

    rows_dev = NCH * RPC
    size = rows_dev * STEPS
    order = iota((size, size), 0)
    source = (order % rows_dev) * STEPS + order // rows_dev
    perm = jnp.where(iota((size, size), 1) == source, 1.0, 0.0).astype(BF16)
    fresh = jnp.dot(perm, kvs[...], preferred_element_type=F32).astype(BF16)
    kv_ref[0] = fresh[:, :HD]
    kv_ref[1] = fresh[:, HD:]

    load_o.wait()
    a5 = send_5a(0, a4)
    a5 = send_5b(0, a5)
    b5 = send_5a(1, b4)
    b5 = send_5b(1, b5)
    finish(0, a5)
    finish(1, b5)

    size = NCH * SL
    order = iota((size, size), 0)
    step, row = order // 8, order % 8
    source = ((row // RPC) % NCH) * SL + (row // (RPC * NCH)) * TPD + (row % RPC) * STEPS + step
    perm = jnp.where(iota((size, size), 1) == source, 1.0, 0.0).astype(BF16)
    out_ref[...] = jnp.dot(perm, fin[...], preferred_element_type=F32).astype(BF16)

    for copy in sends:
        copy.wait_send()


COPIES = NCH * (1 + 3 + 3 + 4 + 9 + 9 + 6 + 6 + 1 + 3)


def body(
    token_ids, cache_lengths, embed_table, norm_gain, qkv_weight, key_cache, value_cache, out_weight
):
    vocab, feats = embed_table.shape
    cols = qkv_weight.shape[1]
    width, out_cols = out_weight.shape
    frequency = THETA ** (-np.arange(HD // 2, dtype=np.float64) * (2.0 / HD))
    frequency = np.concatenate([frequency, frequency]).astype(np.float32)[None, :]
    vmem = pl.BlockSpec(memory_space=pltpu.VMEM)
    hbm = pl.BlockSpec(memory_space=pl.ANY)
    smem = pl.BlockSpec(memory_space=pltpu.SMEM)
    dma = pltpu.SemaphoreType.DMA
    half = cols // 2
    out, kv = pl.pallas_call(
        kernel,
        out_shape=(
            jax.ShapeDtypeStruct((NCH * SL, out_cols), BF16),
            jax.ShapeDtypeStruct((2, NCH * TPD, HD), BF16),
        ),
        in_specs=[vmem, smem, vmem, vmem, hbm, hbm, hbm, hbm, hbm],
        out_specs=(vmem, vmem),
        scratch_shapes=[
            pltpu.VMEM((vocab // TBLK, TBLK, feats), BF16),
            pltpu.VMEM(qkv_weight.shape, BF16),
            pltpu.VMEM(out_weight.shape, BF16),
            pltpu.VMEM(key_cache.shape, BF16),
            pltpu.VMEM(value_cache.shape, BF16),
            pltpu.VMEM((TOK, feats), F32),
            pltpu.VMEM((NCH, 4, 2, SL, feats), BF16),
            pltpu.VMEM((NCH, 4, SL, feats), BF16),
            pltpu.VMEM((NCH, 4, SL, feats), BF16),
            pltpu.VMEM((NCH, 3, SL, feats), BF16),
            pltpu.VMEM((NCH, 4, 2, SL, feats), BF16),
            pltpu.VMEM((NCH, 4, 4, TPD, cols), BF16),
            pltpu.VMEM((NCH, 2, 3, 4, TPD, half), BF16),
            pltpu.VMEM((NCH, 2, 4, TPD, half), BF16),
            pltpu.VMEM((NCH, 2, 3, TPD, half), BF16),
            pltpu.VMEM((NCH, 2, 1, TOK), F32),
            pltpu.VMEM((NCH, 2, 3, 1, TOK), F32),
            pltpu.VMEM((NCH, 4, 4, TPD, width), BF16),
            pltpu.VMEM((NCH, 4, 2, 2, TPD, out_cols), BF16),
            pltpu.VMEM((NCH, 4, 2, TPD, out_cols), BF16),
            pltpu.VMEM((NCH, 4, 2, TPD, out_cols), BF16),
            pltpu.VMEM((NCH, 3, 2, TPD, out_cols), BF16),
            pltpu.VMEM((NCH * SL, out_cols), BF16),
            pltpu.VMEM((NCH * TPD, 2 * HD), BF16),
            dma((2 + 2 * NCH,)),
            dma((vocab // TBLK,)),
            dma((COPIES,)),
            dma((COPIES,)),
        ],
        compiler_params=pltpu.CompilerParams(
            collective_id=0, has_side_effects=True, vmem_limit_bytes=56 << 20
        ),
        cost_estimate=pl.CostEstimate(
            flops=8 * 10**9, bytes_accessed=30 * 10**6, transcendentals=2 * 10**6
        ),
        name="decode_block",
    )(
        token_ids, cache_lengths, norm_gain[None, :], jnp.asarray(frequency), embed_table,
        qkv_weight, key_cache, value_cache, out_weight,
    )
    return (
        out.reshape(STEPS, NCH * SL // STEPS, out_cols),
        kv.reshape(2, STEPS, NCH * RPC, HD),
    )


def solution(mesh):
    in_specs = (
        P(),
        P("gy"),
        P("gx", "gy"),
        P("gy"),
        P("gy", "gx"),
        P("gy", None, "gx"),
        P("gy", None, "gx"),
        P("gx", "gy"),
    )
    out_specs = (P(None, "gx", "gy"), P(None, None, "gy", "gx"))
    return jax.shard_map(body, mesh=mesh, in_specs=in_specs, out_specs=out_specs, check_vma=False)
```

```python
import functools
import math

import jax
import jax.numpy as jnp
import numpy as np
from jax import lax
from jax.experimental import pallas as pl
from jax.experimental.pallas import tpu as pltpu
from jax.sharding import PartitionSpec as P

D = 8192
HD = 128
GROUP = 8
STEPS = 8
THETA = 500000.0
EPS = 1e-05
MASKED = -1e30
MESH = pl.DeviceIdType.MESH

NCH = 2
RPC = 2
TPD = RPC * STEPS
TOK = 16 * TPD
SL = TOK // 8
TBLK = 1024
PBLK = 2048
F32 = jnp.float32
BF16 = jnp.bfloat16


def iota(shape, dim):
    return lax.broadcasted_iota(jnp.int32, shape, dim)


def kernel(
    ids_ref, len_ref, gain_ref, freq_ref, table_hbm, wqkv_hbm, key_hbm, val_hbm, wout_hbm,
    fin, kvs,
    table, wqkv, wout, kbuf, vbuf, acc,
    picks, r1a, s1, r1b, eall, part, ra, sb, rb, sq, rsq, scores, ag, part5, r5a, s5, r5b,
    local_sem, table_sem, send_sem, recv_sem,
):
    gx = lax.axis_index("gx")
    gy = lax.axis_index("gy")
    z, core = gx // 2, gx % 2
    y, x = gy // 4, gy % 4

    def wrap(a, k):
        return (a + k) % 4

    def at_core():
        return (z * 2 + 1 - core, gy)

    def at_z(k):
        return (wrap(z, k) * 2 + core, gy)

    def at_y(k):
        return (gx, wrap(y, k) * 4 + x)

    def at_x(k):
        return (gx, y * 4 + wrap(x, k))

    counter = [0]
    sends = []

    def remote(src, dst, device):
        n = counter[0]
        counter[0] += 1
        copy = pltpu.make_async_remote_copy(
            src_ref=src, dst_ref=dst, send_sem=send_sem.at[n], recv_sem=recv_sem.at[n],
            device_id=device, device_id_type=MESH,
        )
        copy.start()
        sends.append(copy)
        return copy

    nblk = table.shape[0]
    table_copies = []
    for b in range(nblk):
        copy = pltpu.make_async_copy(
            table_hbm.at[pl.ds(b * TBLK, TBLK)], table.at[b], table_sem.at[b]
        )
        copy.start()
        table_copies.append(copy)
    load_w = pltpu.make_async_copy(wqkv_hbm, wqkv, local_sem.at[0])
    load_o = pltpu.make_async_copy(wout_hbm, wout, local_sem.at[1])
    load_kv = []
    for c in range(NCH):
        rows = pl.ds(c * RPC, RPC)
        load_kv.append((
            pltpu.make_async_copy(key_hbm.at[rows], kbuf.at[rows], local_sem.at[2 + 2 * c]),
            pltpu.make_async_copy(val_hbm.at[rows], vbuf.at[rows], local_sem.at[3 + 2 * c]),
        ))

    def start_loads():
        load_w.start()
        for pair in load_kv:
            for copy in pair:
                copy.start()
        load_o.start()

    barrier = pltpu.get_barrier_semaphore()
    partners = [at_core()]
    for k in (1, 2, 3):
        partners += [at_z(k), at_y(k), at_x(k)]
    for device in partners:
        pl.semaphore_signal(barrier, inc=1, device_id=device, device_id_type=MESH)

    ids = ids_ref[...]
    id_high = (ids >> 8).astype(F32).astype(BF16)
    id_low = (ids & 255).astype(F32).astype(BF16)

    def local_ids(c):
        token = iota((TOK, 64), 0)
        row = (token // TPD) * (NCH * RPC) + c * RPC + (token // STEPS) % RPC
        chosen = jnp.where(iota((TOK, 64), 1) == row, 1.0, 0.0).astype(BF16)
        contract = (((1,), (1,)), ((), ()))
        high = lax.dot_general(chosen, id_high, contract, preferred_element_type=F32)
        low = lax.dot_general(chosen, id_low, contract, preferred_element_type=F32)
        both = high * 256.0 + low
        mine = iota((TOK, STEPS), 1) == iota((TOK, STEPS), 0) % STEPS
        column = jnp.sum(jnp.where(mine, both, 0.0), axis=1, keepdims=True)
        return column.astype(jnp.int32) - gx * (nblk * TBLK)

    def gather(c, first):
        local = local_ids(c)
        for b in range(nblk):
            if first:
                table_copies[b].wait()
                if b == nblk - 1:
                    start_loads()
            hot = jnp.where(iota((TOK, TBLK), 1) == local - b * TBLK, 1.0, 0.0).astype(BF16)
            term = jnp.dot(hot, table[b], preferred_element_type=F32)
            if b == 0:
                acc[...] = term
            else:
                acc[...] += term
        picks[c] = acc[...].astype(BF16).reshape(picks.shape[1:])

    def send_1a(c):
        return remote(picks.at[c, :, 1 - core], r1a.at[c], at_core())

    def send_1b(c, copy):
        copy.wait_recv()
        s1[c] = picks[c, :, core] + r1a[c]
        return [remote(s1.at[c, wrap(z, k)], r1b.at[c, k - 1], at_z(k)) for k in (1, 2, 3)]

    def send_1c(c, copies):
        for copy in copies:
            copy.wait_recv()
        eall[c, z, core] = (s1[c, z] + r1b[c, 0]) + (r1b[c, 1] + r1b[c, 2])
        mine = eall.at[c, z, core]
        return (
            [remote(mine, mine, at_z(k)) for k in (1, 2, 3)],
            [remote(mine, mine, at_core())],
        )

    def send_1d(c, copies):
        across, over = copies
        for k, copy in zip((1, 2, 3), across):
            copy.wait_recv()
            block = eall.at[c, wrap(z, 4 - k), core]
            over.append(remote(block, block, at_core()))
        return over

    half = wqkv.shape[1] // 2

    def send_2a(c, copies):
        for copy in copies:
            copy.wait_recv()
        embedded = eall[c].reshape(TOK, eall.shape[-1]).astype(F32)
        scaled = (embedded * gain_ref[...].astype(F32)[None, :]).astype(BF16)
        product = jnp.dot(scaled, wqkv[...], preferred_element_type=F32)
        part[c] = product.astype(BF16).reshape(part.shape[1:])
        out = []
        for k in (1, 2, 3):
            out.append(remote(
                part.at[c, :, wrap(x, k), :, pl.ds(0, half)], ra.at[c, 0, k - 1], at_x(k)
            ))
            out.append(remote(
                part.at[c, wrap(y, k), :, :, pl.ds(half, half)], ra.at[c, 1, k - 1], at_y(k)
            ))
        squares = embedded * embedded
        high = squares.astype(BF16)
        low = (squares - high.astype(F32)).astype(BF16)
        ones = jnp.ones((8, eall.shape[-1]), BF16)
        contract = (((1,), (1,)), ((), ()))
        total = lax.dot_general(ones, high, contract, preferred_element_type=F32)
        total = total + lax.dot_general(ones, low, contract, preferred_element_type=F32)
        sq[c, 0] = total[:1]
        for k in (1, 2, 3):
            out.append(remote(sq.at[c, 0], rsq.at[c, 0, k - 1], at_x(k)))
        return out

    def send_2b(c, copies):
        for copy in copies:
            copy.wait_recv()
        sq[c, 1] = (sq[c, 0] + rsq[c, 0, 0]) + (rsq[c, 0, 1] + rsq[c, 0, 2])
        out = []
        for h, own in ((0, part[c, :, x, :, pl.ds(0, half)]), (1, part[c, y, :, :, pl.ds(half, half)])):
            total = own.astype(F32)
            for k in range(3):
                total = total + ra[c, h, k].astype(F32)
            sb[c, h] = total.astype(BF16)
        for k in (1, 2, 3):
            out.append(remote(sb.at[c, 0, wrap(y, k)], rb.at[c, 0, k - 1], at_y(k)))
            out.append(remote(sb.at[c, 1, wrap(x, k)], rb.at[c, 1, k - 1], at_x(k)))
            out.append(remote(sq.at[c, 1], rsq.at[c, 1, k - 1], at_y(k)))
        return out

    def queries(c, copies):
        for copy in copies:
            copy.wait_recv()
        squares = (sq[c, 1] + rsq[c, 1, 0]) + (rsq[c, 1, 1] + rsq[c, 1, 2])
        place = iota((TPD, TOK), 1) == iota((TPD, TOK), 0) + gy * TPD
        column = jnp.sum(jnp.where(place, squares, 0.0), axis=1, keepdims=True)
        inverse_rms = lax.rsqrt(column / D + EPS)
        pieces = []
        for h, own in ((0, sb[c, 0, y]), (1, sb[c, 1, x])):
            total = own.astype(F32)
            for k in range(3):
                total = total + rb[c, h, k].astype(F32)
            pieces.append(total)
        projected = jnp.concatenate(pieces, axis=1) * inverse_rms
        sub = iota((TPD, 1), 0)
        length = jnp.where(sub < STEPS, len_ref[c * RPC], len_ref[c * RPC + 1])
        position = (length + sub % STEPS).astype(F32)
        angle = position * freq_ref[...]
        cosine = jnp.cos(angle)
        sine = jnp.sin(angle)
        sine = jnp.where(iota((TPD, HD), 1) < HD // 2, -sine, sine)

        def rotate(g):
            field = projected[:, g * HD : (g + 1) * HD]
            return field * cosine + pltpu.roll(field, HD // 2, 1) * sine

        heads = [rotate(g) * HD ** (-0.5) for g in range(GROUP)]
        new_key = rotate(GROUP).astype(BF16)
        new_value = projected[:, (GROUP + 1) * HD :].astype(BF16)
        kvs[pl.ds(c * TPD, TPD)] = jnp.concatenate([new_key, new_value], axis=1)
        rows = [
            jnp.concatenate([head[r * STEPS : (r + 1) * STEPS] for head in heads], axis=0)
            for r in range(RPC)
        ]
        return rows, new_key, new_value

    nq = GROUP * STEPS

    def attention_scores(c, rows, new_key):
        plain = jnp.concatenate(rows, axis=0).astype(BF16)
        nothing = jnp.zeros_like(rows[0])
        paired = jnp.concatenate(
            [
                jnp.concatenate([rows[0], nothing], axis=1),
                jnp.concatenate([nothing, rows[1]], axis=1),
            ],
            axis=0,
        ).astype(BF16)
        fresh = lax.dot_general(
            plain, new_key, (((1,), (1,)), ((), ())), preferred_element_type=F32
        )
        query = iota(fresh.shape, 0)
        entry = iota(fresh.shape, 1)
        allowed = (entry // STEPS == query // nq) & (entry % STEPS <= query % STEPS)
        fresh = jnp.where(allowed, fresh, MASKED)
        r = c * RPC
        limits = (len_ref[r], len_ref[r + 1])

        def step(b, largest):
            start = pl.multiple_of(b * PBLK, PBLK)
            where = pl.ds(start, PBLK)
            keys = jnp.concatenate([kbuf[r, where], kbuf[r + 1, where]], axis=1)
            block = lax.dot_general(
                paired, keys, (((1,), (1,)), ((), ())), preferred_element_type=F32
            )
            place = iota((nq, PBLK), 1) + start
            block = jnp.concatenate(
                [
                    jnp.where(place < limits[0], block[:nq], MASKED),
                    jnp.where(place < limits[1], block[nq:], MASKED),
                ],
                axis=0,
            )
            scores[b] = block
            for n in range(0, PBLK, HD):
                largest = jnp.maximum(largest, block[:, n : n + HD])
            return largest

        largest = lax.fori_loop(
            0, scores.shape[0], step, jnp.full((RPC * nq, HD), MASKED, F32), unroll=2
        )
        largest = jnp.maximum(
            jnp.max(largest, axis=1, keepdims=True), jnp.max(fresh, axis=1, keepdims=True)
        )
        return allowed, fresh, largest

    def attention_values(c, state, new_value):
        allowed, fresh, largest = state
        r = c * RPC
        fresh = jnp.where(allowed, jnp.exp(fresh - largest), 0.0)
        fresh_total = jnp.sum(fresh, axis=1, keepdims=True)
        value = jnp.dot(fresh.astype(BF16), new_value, preferred_element_type=F32)
        level = jnp.broadcast_to(largest, (RPC * nq, HD))

        def step(b, state):
            total, value = state
            where = pl.ds(pl.multiple_of(b * PBLK, PBLK), PBLK)
            pieces = []
            for n in range(0, PBLK, HD):
                piece = jnp.exp(scores[b, :, n : n + HD] - level)
                total = total + piece
                pieces.append(piece.astype(BF16))
            weights = jnp.concatenate(pieces, axis=1)
            values = jnp.concatenate([vbuf[r, where], vbuf[r + 1, where]], axis=1)
            value = value + jnp.dot(weights, values, preferred_element_type=F32)
            return total, value

        total, value = lax.fori_loop(
            0, scores.shape[0], step,
            (jnp.zeros((RPC * nq, HD), F32), jnp.concatenate([value, value], axis=1)), unroll=2,
        )
        return jnp.sum(total, axis=1, keepdims=True) + fresh_total, value

    def send_4a(c, state):
        total, value = state
        value = value / total
        columns = []
        for g in range(GROUP):
            columns.append(jnp.concatenate(
                [
                    value[r * nq + g * STEPS : r * nq + (g + 1) * STEPS, r * HD : (r + 1) * HD]
                    for r in range(RPC)
                ],
                axis=0,
            ))
        ag[c, 0, 0] = jnp.concatenate(columns, axis=1).astype(BF16)
        own = ag.at[c, 0, 0]
        out = ([], [])
        for k in (1, 2, 3):
            out[0].append(remote(own, ag.at[c, 0, k], at_x(k)))
            out[1].append(remote(own, ag.at[c, k, 0], at_y(k)))
        return out

    ahalf = wout.shape[0] // 2

    def send_4b(c, copies):
        along_x, along_y = copies
        out = []
        left, right = pl.ds(0, ahalf), pl.ds(ahalf, ahalf)
        others = pl.ds(1, 3)
        for copy in along_x:
            copy.wait_recv()
        for k in (1, 2, 3):
            out.append(remote(
                ag.at[c, 0, others, :, left], ag.at[c, k, others, :, left], at_y(k)
            ))
        for copy in along_y:
            copy.wait_recv()
        for k in (1, 2, 3):
            out.append(remote(
                ag.at[c, others, 0, :, right], ag.at[c, others, k, :, right], at_x(k)
            ))
        return out

    def send_5a(c, copies):
        for copy in copies:
            copy.wait_recv()
        everyone = ag[c].reshape(TOK, wout.shape[0])
        product = jnp.dot(everyone, wout[...], preferred_element_type=F32).astype(BF16)
        for ky in range(4):
            for kx in range(4):
                n = (ky * 4 + kx) * TPD
                place = wrap(x, 4 - kx)
                part5[c, wrap(y, 4 - ky), place // 2, place % 2] = product[n : n + TPD]
        return remote(part5.at[c, :, 1 - core], r5a.at[c], at_core())

    def send_5b(c, copy):
        copy.wait_recv()
        s5[c] = (part5[c, :, core].astype(F32) + r5a[c].astype(F32)).astype(BF16)
        return [remote(s5.at[c, wrap(z, k)], r5b.at[c, k - 1], at_z(k)) for k in (1, 2, 3)]

    def finish(c, copies):
        for copy in copies:
            copy.wait_recv()
        total = s5[c, z].astype(F32)
        for k in range(3):
            total = total + r5b[c, k].astype(F32)
        fin[pl.ds(c * SL, SL)] = total.astype(BF16).reshape(SL, total.shape[-1])

    gather(0, True)
    pl.semaphore_wait(barrier, len(partners))
    a1 = send_1a(0)
    gather(1, False)
    b1 = send_1a(1)
    a1 = send_1b(0, a1)
    b1 = send_1b(1, b1)
    a1 = send_1c(0, a1)
    b1 = send_1c(1, b1)
    a1 = send_1d(0, a1)
    load_w.wait()
    b1 = send_1d(1, b1)
    a2 = send_2a(0, a1)
    b2 = send_2a(1, b1)
    a2 = send_2b(0, a2)
    b2 = send_2b(1, b2)
    a_rows, a_key, a_value = queries(0, a2)
    for copy in load_kv[0]:
        copy.wait()
    state = attention_scores(0, a_rows, a_key)
    a4 = send_4a(0, attention_values(0, state, a_value))
    b_rows, b_key, b_value = queries(1, b2)
    for copy in load_kv[1]:
        copy.wait()
    state = attention_scores(1, b_rows, b_key)
    a4 = send_4b(0, a4)
    b4 = send_4a(1, attention_values(1, state, b_value))
    b4 = send_4b(1, b4)

    load_o.wait()
    a5 = send_5a(0, a4)
    a5 = send_5b(0, a5)
    b5 = send_5a(1, b4)
    b5 = send_5b(1, b5)
    finish(0, a5)
    finish(1, b5)

    for copy in sends:
        copy.wait_send()


def order_outputs(fin, kvs, out_ref, kv_ref):
    rows_dev = NCH * RPC
    size = rows_dev * STEPS
    order = iota((size, size), 0)
    source = (order % rows_dev) * STEPS + order // rows_dev
    perm = jnp.where(iota((size, size), 1) == source, 1.0, 0.0).astype(BF16)
    fresh = jnp.dot(perm, kvs[...], preferred_element_type=F32).astype(BF16)
    kv_ref[0] = fresh[:, :HD]
    kv_ref[1] = fresh[:, HD:]


    size = NCH * SL
    order = iota((size, size), 0)
    step, row = order // 8, order % 8
    source = ((row // RPC) % NCH) * SL + (row // (RPC * NCH)) * TPD + (row % RPC) * STEPS + step
    perm = jnp.where(iota((size, size), 1) == source, 1.0, 0.0).astype(BF16)
    out_ref[...] = jnp.dot(perm, fin[...], preferred_element_type=F32).astype(BF16)


COPIES = NCH * (1 + 3 + 3 + 4 + 9 + 9 + 6 + 6 + 1 + 3)


def body(
    token_ids, cache_lengths, embed_table, norm_gain, qkv_weight, key_cache, value_cache, out_weight
):
    vocab, feats = embed_table.shape
    cols = qkv_weight.shape[1]
    width, out_cols = out_weight.shape
    frequency = THETA ** (-np.arange(HD // 2, dtype=np.float64) * (2.0 / HD))
    frequency = np.concatenate([frequency, frequency]).astype(np.float32)[None, :]
    vmem = pl.BlockSpec(memory_space=pltpu.VMEM)
    hbm = pl.BlockSpec(memory_space=pl.ANY)
    smem = pl.BlockSpec(memory_space=pltpu.SMEM)
    dma = pltpu.SemaphoreType.DMA
    half = cols // 2
    fin, kvs = pl.pallas_call(
        kernel,
        out_shape=(
            jax.ShapeDtypeStruct((NCH * SL, out_cols), BF16),
            jax.ShapeDtypeStruct((NCH * TPD, 2 * HD), BF16),
        ),
        in_specs=[vmem, smem, vmem, vmem, hbm, hbm, hbm, hbm, hbm],
        out_specs=(vmem, vmem),
        scratch_shapes=[
            pltpu.VMEM((vocab // TBLK, TBLK, feats), BF16),
            pltpu.VMEM(qkv_weight.shape, BF16),
            pltpu.VMEM(out_weight.shape, BF16),
            pltpu.VMEM(key_cache.shape, BF16),
            pltpu.VMEM(value_cache.shape, BF16),
            pltpu.VMEM((TOK, feats), F32),
            pltpu.VMEM((NCH, 4, 2, SL, feats), BF16),
            pltpu.VMEM((NCH, 4, SL, feats), BF16),
            pltpu.VMEM((NCH, 4, SL, feats), BF16),
            pltpu.VMEM((NCH, 3, SL, feats), BF16),
            pltpu.VMEM((NCH, 4, 2, SL, feats), BF16),
            pltpu.VMEM((NCH, 4, 4, TPD, cols), BF16),
            pltpu.VMEM((NCH, 2, 3, 4, TPD, half), BF16),
            pltpu.VMEM((NCH, 2, 4, TPD, half), BF16),
            pltpu.VMEM((NCH, 2, 3, TPD, half), BF16),
            pltpu.VMEM((NCH, 2, 1, TOK), F32),
            pltpu.VMEM((NCH, 2, 3, 1, TOK), F32),
            pltpu.VMEM((key_cache.shape[1] // PBLK, RPC * GROUP * STEPS, PBLK), F32),
            pltpu.VMEM((NCH, 4, 4, TPD, width), BF16),
            pltpu.VMEM((NCH, 4, 2, 2, TPD, out_cols), BF16),
            pltpu.VMEM((NCH, 4, 2, TPD, out_cols), BF16),
            pltpu.VMEM((NCH, 4, 2, TPD, out_cols), BF16),
            pltpu.VMEM((NCH, 3, 2, TPD, out_cols), BF16),
            dma((2 + 2 * NCH,)),
            dma((vocab // TBLK,)),
            dma((COPIES,)),
            dma((COPIES,)),
        ],
        compiler_params=pltpu.CompilerParams(
            collective_id=0, has_side_effects=True, vmem_limit_bytes=56 << 20
        ),
        cost_estimate=pl.CostEstimate(
            flops=8 * 10**9, bytes_accessed=30 * 10**6, transcendentals=2 * 10**6
        ),
        name="decode_block",
    )(
        token_ids, cache_lengths, norm_gain, jnp.asarray(frequency), embed_table,
        qkv_weight, key_cache, value_cache, out_weight,
    )
    out, kv = pl.pallas_call(
        order_outputs,
        out_shape=(
            jax.ShapeDtypeStruct((NCH * SL, out_cols), BF16),
            jax.ShapeDtypeStruct((2, NCH * TPD, HD), BF16),
        ),
        in_specs=[vmem, vmem],
        out_specs=(vmem, vmem),
        name="order_outputs",
    )(fin, kvs)
    return (
        out.reshape(STEPS, NCH * SL // STEPS, out_cols),
        kv.reshape(2, STEPS, NCH * RPC, HD),
    )


def solution(mesh):
    in_specs = (
        P(),
        P("gy"),
        P("gx", "gy"),
        P("gy"),
        P("gy", "gx"),
        P("gy", None, "gx"),
        P("gy", None, "gx"),
        P("gx", "gy"),
    )
    out_specs = (P(None, "gx", "gy"), P(None, None, "gy", "gx"))
    return jax.shard_map(body, mesh=mesh, in_specs=in_specs, out_specs=out_specs, check_vma=False)
```

```python
import functools
import math

import jax
import jax.numpy as jnp
import numpy as np
from jax import lax
from jax.experimental import pallas as pl
from jax.experimental.pallas import tpu as pltpu
from jax.sharding import PartitionSpec as P

D = 8192
HD = 128
GROUP = 8
STEPS = 8
THETA = 500000.0
EPS = 1e-05
MASKED = -1e30
MESH = pl.DeviceIdType.MESH

NCH = 2
RPC = 2
TPD = RPC * STEPS
TOK = 16 * TPD
SL = TOK // 8
TBLK = 2048
PBLK = 4096
TURN = 1024
F32 = jnp.float32
BF16 = jnp.bfloat16


def iota(shape, dim):
    return lax.broadcasted_iota(jnp.int32, shape, dim)


def kernel(
    len_ref, ids_hbm, gain_hbm, freq_hbm, table_hbm, wqkv_hbm, key_hbm, val_hbm, wout_hbm,
    fin, kvs,
    ids_ref, gain_ref, freq_ref, table, wqkv, wout, kbuf, kturned, vbuf, acc,
    picks, r1a, s1, r1b, eall, part, ra, sb, rb, sq, rsq, scores, ag, part5, r5a, s5, r5b,
    small_sem, local_sem, table_sem, send_sem, recv_sem,
):
    gx = lax.axis_index("gx")
    gy = lax.axis_index("gy")
    z, core = gx // 2, gx % 2
    y, x = gy // 4, gy % 4

    def wrap(a, k):
        return (a + k) % 4

    def at_core():
        return (z * 2 + 1 - core, gy)

    def at_z(k):
        return (wrap(z, k) * 2 + core, gy)

    def at_y(k):
        return (gx, wrap(y, k) * 4 + x)

    def at_x(k):
        return (gx, y * 4 + wrap(x, k))

    counter = [0]
    sends = []

    def remote(src, dst, device):
        n = counter[0]
        counter[0] += 1
        copy = pltpu.make_async_remote_copy(
            src_ref=src, dst_ref=dst, send_sem=send_sem.at[n], recv_sem=recv_sem.at[n],
            device_id=device, device_id_type=MESH,
        )
        copy.start()
        sends.append(copy)
        return copy

    small = [
        pltpu.make_async_copy(hbm, ref, small_sem.at[n])
        for n, (hbm, ref) in enumerate(
            ((ids_hbm, ids_ref), (gain_hbm, gain_ref), (freq_hbm, freq_ref))
        )
    ]
    for copy in small:
        copy.start()
    nblk = table.shape[0]
    table_copies = []
    for b in range(nblk):
        copy = pltpu.make_async_copy(
            table_hbm.at[pl.ds(b * TBLK, TBLK)], table.at[b], table_sem.at[b]
        )
        copy.start()
        table_copies.append(copy)
    load_w = pltpu.make_async_copy(wqkv_hbm, wqkv, local_sem.at[0])
    load_o = pltpu.make_async_copy(wout_hbm, wout, local_sem.at[1])
    load_kv = []
    for c in range(NCH):
        rows = pl.ds(c * RPC, RPC)
        load_kv.append((
            pltpu.make_async_copy(key_hbm.at[rows], kbuf.at[rows], local_sem.at[2 + 2 * c]),
            pltpu.make_async_copy(val_hbm.at[rows], vbuf.at[rows], local_sem.at[3 + 2 * c]),
        ))

    def start_loads():
        load_w.start()
        for pair in load_kv:
            for copy in pair:
                copy.start()
        load_o.start()

    barrier = pltpu.get_barrier_semaphore()
    partners = [at_core()]
    for k in (1, 2, 3):
        partners += [at_z(k), at_y(k), at_x(k)]
    for device in partners:
        pl.semaphore_signal(barrier, inc=1, device_id=device, device_id_type=MESH)

    for copy in small:
        copy.wait()
    ids = ids_ref[...]
    id_high = (ids >> 8).astype(F32).astype(BF16)
    id_low = (ids & 255).astype(F32).astype(BF16)

    def local_ids(c):
        token = iota((TOK, 64), 0)
        row = (token // TPD) * (NCH * RPC) + c * RPC + (token // STEPS) % RPC
        chosen = jnp.where(iota((TOK, 64), 1) == row, 1.0, 0.0).astype(BF16)
        contract = (((1,), (1,)), ((), ()))
        high = lax.dot_general(chosen, id_high, contract, preferred_element_type=F32)
        low = lax.dot_general(chosen, id_low, contract, preferred_element_type=F32)
        both = high * 256.0 + low
        mine = iota((TOK, STEPS), 1) == iota((TOK, STEPS), 0) % STEPS
        column = jnp.sum(jnp.where(mine, both, 0.0), axis=1, keepdims=True)
        return column.astype(jnp.int32) - gx * (nblk * TBLK)

    local = [local_ids(c) for c in range(NCH)]

    def gather(c, b):
        hot = jnp.where(iota((TOK, TBLK), 1) == local[c] - b * TBLK, 1.0, 0.0).astype(BF16)
        term = jnp.dot(hot, table[b], preferred_element_type=F32)
        if b == 0:
            acc[c] = term
        elif b < nblk - 1:
            acc[c] += term
        else:
            picks[c] = (acc[c] + term).astype(BF16).reshape(picks.shape[1:])

    def send_1a(c):
        return remote(picks.at[c, :, 1 - core], r1a.at[c], at_core())

    def send_1b(c, copy):
        copy.wait_recv()
        s1[c] = picks[c, :, core] + r1a[c]
        return [remote(s1.at[c, wrap(z, k)], r1b.at[c, k - 1], at_z(k)) for k in (1, 2, 3)]

    def send_1c(c, copies):
        for copy in copies:
            copy.wait_recv()
        eall[c, z, core] = (s1[c, z] + r1b[c, 0]) + (r1b[c, 1] + r1b[c, 2])
        mine = eall.at[c, z, core]
        return (
            [remote(mine, mine, at_z(k)) for k in (1, 2, 3)],
            [remote(mine, mine, at_core())],
        )

    def send_1d(c, copies):
        across, over = copies
        for k, copy in zip((1, 2, 3), across):
            copy.wait_recv()
            block = eall.at[c, wrap(z, 4 - k), core]
            over.append(remote(block, block, at_core()))
        return over

    half = wqkv.shape[1] // 2

    def send_2a(c, copies):
        for copy in copies:
            copy.wait_recv()
        embedded = eall[c].reshape(TOK, eall.shape[-1]).astype(F32)
        scaled = (embedded * gain_ref[...].astype(F32)[None, :]).astype(BF16)
        out = []
        for h in range(2):
            own = pl.ds(h * half, half)
            product = jnp.dot(scaled, wqkv[:, own], preferred_element_type=F32)
            part[c, :, :, :, own] = product.astype(BF16).reshape(4, 4, TPD, half)
            for k in (1, 2, 3):
                if h == 0:
                    block, device = part.at[c, :, wrap(x, k), :, own], at_x(k)
                else:
                    block, device = part.at[c, wrap(y, k), :, :, own], at_y(k)
                out.append(remote(block, ra.at[c, h, k - 1], device))
        squares = embedded * embedded
        high = squares.astype(BF16)
        low = (squares - high.astype(F32)).astype(BF16)
        ones = jnp.ones((8, eall.shape[-1]), BF16)
        contract = (((1,), (1,)), ((), ()))
        total = lax.dot_general(ones, high, contract, preferred_element_type=F32)
        total = total + lax.dot_general(ones, low, contract, preferred_element_type=F32)
        sq[c, 0] = total[:1]
        for k in (1, 2, 3):
            out.append(remote(sq.at[c, 0], rsq.at[c, 0, k - 1], at_x(k)))
        return out

    def send_2b(c, copies):
        for copy in copies:
            copy.wait_recv()
        sq[c, 1] = (sq[c, 0] + rsq[c, 0, 0]) + (rsq[c, 0, 1] + rsq[c, 0, 2])
        out = []
        for h, own in ((0, part[c, :, x, :, pl.ds(0, half)]), (1, part[c, y, :, :, pl.ds(half, half)])):
            total = own.astype(F32)
            for k in range(3):
                total = total + ra[c, h, k].astype(F32)
            sb[c, h] = total.astype(BF16)
            for k in (1, 2, 3):
                if h == 0:
                    out.append(remote(sb.at[c, 0, wrap(y, k)], rb.at[c, 0, k - 1], at_y(k)))
                    out.append(remote(sq.at[c, 1], rsq.at[c, 1, k - 1], at_y(k)))
                else:
                    out.append(remote(sb.at[c, 1, wrap(x, k)], rb.at[c, 1, k - 1], at_x(k)))
        return out

    def queries(c, copies):
        for copy in copies:
            copy.wait_recv()
        squares = (sq[c, 1] + rsq[c, 1, 0]) + (rsq[c, 1, 1] + rsq[c, 1, 2])
        place = iota((TPD, TOK), 1) == iota((TPD, TOK), 0) + gy * TPD
        column = jnp.sum(jnp.where(place, squares, 0.0), axis=1, keepdims=True)
        inverse_rms = lax.rsqrt(column / D + EPS)
        pieces = []
        for h, own in ((0, sb[c, 0, y]), (1, sb[c, 1, x])):
            total = own.astype(F32)
            for k in range(3):
                total = total + rb[c, h, k].astype(F32)
            pieces.append(total)
        projected = jnp.concatenate(pieces, axis=1) * inverse_rms
        sub = iota((TPD, 1), 0)
        length = jnp.where(sub < STEPS, len_ref[c * RPC], len_ref[c * RPC + 1])
        position = (length + sub % STEPS).astype(F32)
        angle = position * freq_ref[...]
        cosine = jnp.cos(angle)
        sine = jnp.sin(angle)
        sine = jnp.where(iota((TPD, HD), 1) < HD // 2, -sine, sine)

        def rotate(g):
            field = projected[:, g * HD : (g + 1) * HD]
            return field * cosine + pltpu.roll(field, HD // 2, 1) * sine

        heads = [rotate(g) * HD ** (-0.5) for g in range(GROUP)]
        new_key = rotate(GROUP).astype(BF16)
        new_value = projected[:, (GROUP + 1) * HD :].astype(BF16)
        kvs[pl.ds(c * TPD, TPD)] = jnp.concatenate([new_key, new_value], axis=1)
        rows = [
            jnp.concatenate([head[r * STEPS : (r + 1) * STEPS] for head in heads], axis=0)
            for r in range(RPC)
        ]
        return jnp.concatenate(rows, axis=0).astype(BF16), new_key, new_value

    nq = GROUP * STEPS

    def turn_keys(c):
        for copy in load_kv[c]:
            copy.wait()

        @pl.loop(0, RPC * kbuf.shape[1] // TURN, unroll=2)
        def _(n):
            per_row = kbuf.shape[1] // TURN
            r = c * RPC + n // per_row
            where = pl.ds(pl.multiple_of(n % per_row * TURN, TURN), TURN)
            kturned[r, :, where] = kbuf[r, where].T

    def attention_scores(c, query, new_key):
        fresh = lax.dot_general(
            query, new_key, (((1,), (1,)), ((), ())), preferred_element_type=F32
        )
        ask = iota(fresh.shape, 0)
        entry = iota(fresh.shape, 1)
        allowed = (entry // STEPS == ask // nq) & (entry % STEPS <= ask % STEPS)
        fresh = jnp.where(allowed, fresh, MASKED)

        def step(b, largest):
            start = pl.multiple_of(b * PBLK, PBLK)
            where = pl.ds(start, PBLK)
            place = iota((nq, PBLK), 1) + start
            larger = []
            for i in range(RPC):
                own = slice(i * nq, (i + 1) * nq)
                block = jnp.dot(
                    query[own], kturned[c * RPC + i, :, where], preferred_element_type=F32
                )
                block = jnp.where(place < len_ref[c * RPC + i], block, MASKED)
                scores[b, own] = block
                top = largest[i]
                for n in range(0, PBLK, HD):
                    top = jnp.maximum(top, block[:, n : n + HD])
                larger.append(top)
            return tuple(larger)

        least = jnp.full((nq, HD), MASKED, F32)
        largest = lax.fori_loop(0, scores.shape[0], step, (least,) * RPC, unroll=2)
        largest = jnp.concatenate(largest, axis=0)
        largest = jnp.maximum(
            jnp.max(largest, axis=1, keepdims=True), jnp.max(fresh, axis=1, keepdims=True)
        )
        return allowed, fresh, largest

    def attention_values(c, state, new_value):
        allowed, fresh, largest = state
        fresh = jnp.where(allowed, jnp.exp(fresh - largest), 0.0)
        fresh_total = jnp.sum(fresh, axis=1, keepdims=True)
        fresh_value = jnp.dot(fresh.astype(BF16), new_value, preferred_element_type=F32)
        level = jnp.broadcast_to(largest, (RPC * nq, HD))

        def step(b, state):
            where = pl.ds(pl.multiple_of(b * PBLK, PBLK), PBLK)
            later = []
            for i in range(RPC):
                own = slice(i * nq, (i + 1) * nq)
                total, value = state[i]
                pieces = []
                for n in range(0, PBLK, HD):
                    piece = jnp.exp(scores[b, own, n : n + HD] - level[own])
                    total = total + piece
                    pieces.append(piece.astype(BF16))
                weights = jnp.concatenate(pieces, axis=1)
                value = value + jnp.dot(
                    weights, vbuf[c * RPC + i, where], preferred_element_type=F32
                )
                later.append((total, value))
            return tuple(later)

        nothing = jnp.zeros((nq, HD), F32)
        result = lax.fori_loop(
            0, scores.shape[0], step, ((nothing, nothing),) * RPC, unroll=2
        )
        total = jnp.concatenate([total for total, _ in result], axis=0)
        value = jnp.concatenate([value for _, value in result], axis=0)
        return jnp.sum(total, axis=1, keepdims=True) + fresh_total, value + fresh_value

    def send_4a(c, state):
        total, value = state
        value = value / total
        columns = []
        for g in range(GROUP):
            columns.append(jnp.concatenate(
                [
                    value[r * nq + g * STEPS : r * nq + (g + 1) * STEPS]
                    for r in range(RPC)
                ],
                axis=0,
            ))
        ag[c, 0, 0] = jnp.concatenate(columns, axis=1).astype(BF16)
        own = ag.at[c, 0, 0]
        out = ([], [])
        for k in (1, 2, 3):
            out[0].append(remote(own, ag.at[c, 0, k], at_x(k)))
            out[1].append(remote(own, ag.at[c, k, 0], at_y(k)))
        return out

    ahalf = wout.shape[0] // 2

    def send_4b(c, copies):
        along_x, along_y = copies
        out = []
        left, right = pl.ds(0, ahalf), pl.ds(ahalf, ahalf)
        others = pl.ds(1, 3)
        for copy in along_x:
            copy.wait_recv()
        for k in (1, 2, 3):
            out.append(remote(
                ag.at[c, 0, others, :, left], ag.at[c, k, others, :, left], at_y(k)
            ))
        for copy in along_y:
            copy.wait_recv()
        for k in (1, 2, 3):
            out.append(remote(
                ag.at[c, others, 0, :, right], ag.at[c, others, k, :, right], at_x(k)
            ))
        return out

    def send_5a(c, copies):
        for copy in copies:
            copy.wait_recv()
        everyone = ag[c].reshape(TOK, wout.shape[0])
        product = jnp.dot(everyone, wout[...], preferred_element_type=F32).astype(BF16)
        for ky in range(4):
            for kx in range(4):
                n = (ky * 4 + kx) * TPD
                place = wrap(x, 4 - kx)
                part5[c, wrap(y, 4 - ky), place // 2, place % 2] = product[n : n + TPD]
        return remote(part5.at[c, :, 1 - core], r5a.at[c], at_core())

    def send_5b(c, copy):
        copy.wait_recv()
        s5[c] = (part5[c, :, core].astype(F32) + r5a[c].astype(F32)).astype(BF16)
        return [remote(s5.at[c, wrap(z, k)], r5b.at[c, k - 1], at_z(k)) for k in (1, 2, 3)]

    def finish(c, copies):
        for copy in copies:
            copy.wait_recv()
        total = s5[c, z].astype(F32)
        for k in range(3):
            total = total + r5b[c, k].astype(F32)
        fin[pl.ds(c * SL, SL)] = total.astype(BF16).reshape(SL, total.shape[-1])

    for b in range(nblk):
        table_copies[b].wait()
        if b == nblk - 1:
            start_loads()
        gather(0, b)
    pl.semaphore_wait(barrier, len(partners))
    a1 = send_1a(0)
    for b in range(nblk // 2):
        gather(1, b)
    a1 = send_1b(0, a1)
    for b in range(nblk // 2, nblk):
        gather(1, b)
    b1 = send_1a(1)
    b1 = send_1b(1, b1)
    a1 = send_1c(0, a1)
    b1 = send_1c(1, b1)
    a1 = send_1d(0, a1)
    load_w.wait()
    a2 = send_2a(0, a1)
    b1 = send_1d(1, b1)
    b2 = send_2a(1, b1)
    turn_keys(0)
    a2 = send_2b(0, a2)
    turn_keys(1)
    b2 = send_2b(1, b2)
    a_rows, a_key, a_value = queries(0, a2)
    state = attention_scores(0, a_rows, a_key)
    a4 = send_4a(0, attention_values(0, state, a_value))
    b_rows, b_key, b_value = queries(1, b2)
    state = attention_scores(1, b_rows, b_key)
    b4 = send_4a(1, attention_values(1, state, b_value))
    a4 = send_4b(0, a4)
    b4 = send_4b(1, b4)

    load_o.wait()
    a5 = send_5a(0, a4)
    a5 = send_5b(0, a5)
    b5 = send_5a(1, b4)
    b5 = send_5b(1, b5)
    finish(0, a5)
    finish(1, b5)

    for copy in sends:
        copy.wait_send()


def order_outputs(fin, kvs, out_ref, kv_ref):
    rows_dev = NCH * RPC
    size = rows_dev * STEPS
    order = iota((size, size), 0)
    source = (order % rows_dev) * STEPS + order // rows_dev
    perm = jnp.where(iota((size, size), 1) == source, 1.0, 0.0).astype(BF16)
    fresh = jnp.dot(perm, kvs[...], preferred_element_type=F32).astype(BF16)
    kv_ref[0] = fresh[:, :HD]
    kv_ref[1] = fresh[:, HD:]


    size = NCH * SL
    order = iota((size, size), 0)
    step, row = order // 8, order % 8
    source = ((row // RPC) % NCH) * SL + (row // (RPC * NCH)) * TPD + (row % RPC) * STEPS + step
    perm = jnp.where(iota((size, size), 1) == source, 1.0, 0.0).astype(BF16)
    out_ref[...] = jnp.dot(perm, fin[...], preferred_element_type=F32).astype(BF16)


COPIES = NCH * (1 + 3 + 3 + 4 + 9 + 9 + 6 + 6 + 1 + 3)


def body(
    token_ids, cache_lengths, embed_table, norm_gain, qkv_weight, key_cache, value_cache, out_weight
):
    vocab, feats = embed_table.shape
    cols = qkv_weight.shape[1]
    width, out_cols = out_weight.shape
    frequency = THETA ** (-np.arange(HD // 2, dtype=np.float64) * (2.0 / HD))
    frequency = np.concatenate([frequency, frequency]).astype(np.float32)[None, :]
    vmem = pl.BlockSpec(memory_space=pltpu.VMEM)
    hbm = pl.BlockSpec(memory_space=pl.ANY)
    smem = pl.BlockSpec(memory_space=pltpu.SMEM)
    dma = pltpu.SemaphoreType.DMA
    half = cols // 2
    fin, kvs = pl.pallas_call(
        kernel,
        out_shape=(
            jax.ShapeDtypeStruct((NCH * SL, out_cols), BF16),
            jax.ShapeDtypeStruct((NCH * TPD, 2 * HD), BF16),
        ),
        in_specs=[smem] + [hbm] * 8,
        out_specs=(vmem, vmem),
        scratch_shapes=[
            pltpu.VMEM(token_ids.shape, jnp.int32),
            pltpu.VMEM(norm_gain.shape, BF16),
            pltpu.VMEM(frequency.shape, F32),
            pltpu.VMEM((vocab // TBLK, TBLK, feats), BF16),
            pltpu.VMEM(qkv_weight.shape, BF16),
            pltpu.VMEM(out_weight.shape, BF16),
            pltpu.VMEM(key_cache.shape, BF16),
            pltpu.VMEM((key_cache.shape[0], HD, key_cache.shape[1]), BF16),
            pltpu.VMEM(value_cache.shape, BF16),
            pltpu.VMEM((NCH, TOK, feats), F32),
            pltpu.VMEM((NCH, 4, 2, SL, feats), BF16),
            pltpu.VMEM((NCH, 4, SL, feats), BF16),
            pltpu.VMEM((NCH, 4, SL, feats), BF16),
            pltpu.VMEM((NCH, 3, SL, feats), BF16),
            pltpu.VMEM((NCH, 4, 2, SL, feats), BF16),
            pltpu.VMEM((NCH, 4, 4, TPD, cols), BF16),
            pltpu.VMEM((NCH, 2, 3, 4, TPD, half), BF16),
            pltpu.VMEM((NCH, 2, 4, TPD, half), BF16),
            pltpu.VMEM((NCH, 2, 3, TPD, half), BF16),
            pltpu.VMEM((NCH, 2, 1, TOK), F32),
            pltpu.VMEM((NCH, 2, 3, 1, TOK), F32),
            pltpu.VMEM((key_cache.shape[1] // PBLK, RPC * GROUP * STEPS, PBLK), F32),
            pltpu.VMEM((NCH, 4, 4, TPD, width), BF16),
            pltpu.VMEM((NCH, 4, 2, 2, TPD, out_cols), BF16),
            pltpu.VMEM((NCH, 4, 2, TPD, out_cols), BF16),
            pltpu.VMEM((NCH, 4, 2, TPD, out_cols), BF16),
            pltpu.VMEM((NCH, 3, 2, TPD, out_cols), BF16),
            dma((3,)),
            dma((2 + 2 * NCH,)),
            dma((vocab // TBLK,)),
            dma((COPIES,)),
            dma((COPIES,)),
        ],
        compiler_params=pltpu.CompilerParams(
            collective_id=0, has_side_effects=True, vmem_limit_bytes=56 << 20
        ),
        cost_estimate=pl.CostEstimate(
            flops=8 * 10**9, bytes_accessed=30 * 10**6, transcendentals=2 * 10**6
        ),
        name="decode_block",
    )(
        cache_lengths, token_ids, norm_gain, jnp.asarray(frequency), embed_table,
        qkv_weight, key_cache, value_cache, out_weight,
    )
    out, kv = pl.pallas_call(
        order_outputs,
        out_shape=(
            jax.ShapeDtypeStruct((NCH * SL, out_cols), BF16),
            jax.ShapeDtypeStruct((2, NCH * TPD, HD), BF16),
        ),
        in_specs=[vmem, vmem],
        out_specs=(vmem, vmem),
        name="order_outputs",
    )(fin, kvs)
    return (
        out.reshape(STEPS, NCH * SL // STEPS, out_cols),
        kv.reshape(2, STEPS, NCH * RPC, HD),
    )


def solution(mesh):
    in_specs = (
        P(),
        P("gy"),
        P("gx", "gy"),
        P("gy"),
        P("gy", "gx"),
        P("gy", None, "gx"),
        P("gy", None, "gx"),
        P("gx", "gy"),
    )
    out_specs = (P(None, "gx", "gy"), P(None, None, "gy", "gx"))
    return jax.shard_map(body, mesh=mesh, in_specs=in_specs, out_specs=out_specs, check_vma=False)
```

```python
import functools
import math

import jax
import jax.numpy as jnp
import numpy as np
from jax import lax
from jax.experimental import pallas as pl
from jax.experimental.pallas import tpu as pltpu
from jax.sharding import PartitionSpec as P

D = 8192
HD = 128
GROUP = 8
STEPS = 8
THETA = 500000.0
EPS = 1e-05
MASKED = -1e30
MESH = pl.DeviceIdType.MESH

ROWS = 4
CHUNKS = ((0, 2), (2, 1), (3, 1))
NGR = 2
PARTS = ((0,), (1, 2))
GTOK = 16 * 2 * STEPS
GSL = GTOK // 8
TBLK = 2048
PBLK = 4096
TURN = 1024
F32 = jnp.float32
BF16 = jnp.bfloat16


def iota(shape, dim):
    return lax.broadcasted_iota(jnp.int32, shape, dim)


def kernel(
    len_ref, ids_hbm, gain_hbm, freq_hbm, table_hbm, wqkv_hbm, key_hbm, val_hbm, wout_hbm,
    fin, kvs,
    ids_ref, gain_ref, freq_ref, table, wqkv, wout, kbuf, kturned, vbuf, acc,
    picks, r1a, s1, r1b, eall, scores, turn, chunks,
    small_sem, local_sem, table_sem, send_sem, recv_sem,
):
    gx = lax.axis_index("gx")
    gy = lax.axis_index("gy")
    z, core = gx // 2, gx % 2
    y, x = gy // 4, gy % 4

    def wrap(a, k):
        return (a + k) % 4

    def at_core():
        return (z * 2 + 1 - core, gy)

    def at_z(k):
        return (wrap(z, k) * 2 + core, gy)

    def at_y(k):
        return (gx, wrap(y, k) * 4 + x)

    def at_x(k):
        return (gx, y * 4 + wrap(x, k))

    counter = [0]
    sends = []

    def remote(src, dst, device):
        n = counter[0]
        counter[0] += 1
        copy = pltpu.make_async_remote_copy(
            src_ref=src, dst_ref=dst, send_sem=send_sem.at[n], recv_sem=recv_sem.at[n],
            device_id=device, device_id_type=MESH,
        )
        copy.start()
        sends.append(copy)
        return copy

    small = [
        pltpu.make_async_copy(hbm, ref, small_sem.at[n])
        for n, (hbm, ref) in enumerate(
            ((ids_hbm, ids_ref), (gain_hbm, gain_ref), (freq_hbm, freq_ref))
        )
    ]
    for copy in small:
        copy.start()
    nblk = table.shape[0]
    table_copies = []
    for b in range(nblk):
        copy = pltpu.make_async_copy(
            table_hbm.at[pl.ds(b * TBLK, TBLK)], table.at[b], table_sem.at[b]
        )
        copy.start()
        table_copies.append(copy)
    load_w = pltpu.make_async_copy(wqkv_hbm, wqkv, local_sem.at[0])
    load_o = pltpu.make_async_copy(wout_hbm, wout, local_sem.at[1])
    load_kv = []
    for first, rpc in CHUNKS:
        rows = pl.ds(first, rpc)
        c = len(load_kv)
        load_kv.append((
            pltpu.make_async_copy(key_hbm.at[rows], kbuf.at[rows], local_sem.at[2 + 2 * c]),
            pltpu.make_async_copy(val_hbm.at[rows], vbuf.at[rows], local_sem.at[3 + 2 * c]),
        ))

    def start_loads():
        load_w.start()
        for pair in load_kv:
            for copy in pair:
                copy.start()
        load_o.start()

    barrier = pltpu.get_barrier_semaphore()
    partners = [at_core()]
    for k in (1, 2, 3):
        partners += [at_z(k), at_y(k), at_x(k)]
    for device in partners:
        pl.semaphore_signal(barrier, inc=1, device_id=device, device_id_type=MESH)

    for copy in small:
        copy.wait()
    ids = ids_ref[...]
    id_high = (ids >> 8).astype(F32).astype(BF16)
    id_low = (ids & 255).astype(F32).astype(BF16)

    def local_ids(g):
        first, rpc = CHUNKS[PARTS[g][0]]
        token = iota((GTOK, 64), 0)
        place = token % (16 * rpc * STEPS)
        row = place // (rpc * STEPS) * ROWS + first
        row = row + token // (16 * rpc * STEPS) + place // STEPS % rpc
        chosen = jnp.where(iota((GTOK, 64), 1) == row, 1.0, 0.0).astype(BF16)
        contract = (((1,), (1,)), ((), ()))
        high = lax.dot_general(chosen, id_high, contract, preferred_element_type=F32)
        low = lax.dot_general(chosen, id_low, contract, preferred_element_type=F32)
        both = high * 256.0 + low
        mine = iota((GTOK, STEPS), 1) == iota((GTOK, STEPS), 0) % STEPS
        column = jnp.sum(jnp.where(mine, both, 0.0), axis=1, keepdims=True)
        return column.astype(jnp.int32) - gx * (nblk * TBLK)

    local = [local_ids(g) for g in range(NGR)]

    def gather(c, b):
        hot = jnp.where(iota((GTOK, TBLK), 1) == local[c] - b * TBLK, 1.0, 0.0).astype(BF16)
        term = jnp.dot(hot, table[b], preferred_element_type=F32)
        if b == 0:
            acc[c] = term
        elif b < nblk - 1:
            acc[c] += term
        else:
            picks[c] = (acc[c] + term).astype(BF16).reshape(picks.shape[1:])

    def send_1a(c):
        return remote(picks.at[c, :, 1 - core], r1a.at[c], at_core())

    def send_1b(c, copy):
        copy.wait_recv()
        s1[c] = picks[c, :, core] + r1a[c]
        return [remote(s1.at[c, wrap(z, k)], r1b.at[c, k - 1], at_z(k)) for k in (1, 2, 3)]

    def send_1c(c, copies):
        for copy in copies:
            copy.wait_recv()
        eall[c, z, core] = (s1[c, z] + r1b[c, 0]) + (r1b[c, 1] + r1b[c, 2])
        mine = eall.at[c, z, core]
        return (
            [remote(mine, mine, at_z(k)) for k in (1, 2, 3)],
            [remote(mine, mine, at_core())],
        )

    def send_1d(c, copies):
        across, over = copies
        for k, copy in zip((1, 2, 3), across):
            copy.wait_recv()
            block = eall.at[c, wrap(z, 4 - k), core]
            over.append(remote(block, block, at_core()))
        return over

    half = wqkv.shape[1] // 2

    def send_2a(c):
        rpc = CHUNKS[c][1]
        tok = 16 * rpc * STEPS
        g = 0 if c in PARTS[0] else 1
        size = 4 // len(PARTS[g])
        embedded = eall[g, pl.ds(PARTS[g].index(c) * size, size)]
        embedded = embedded.reshape(tok, eall.shape[-1]).astype(F32)
        scaled = (embedded * gain_ref[...].astype(F32)[None, :]).astype(BF16)
        out = []
        for h in range(2):
            own = pl.ds(h * half, half)
            product = jnp.dot(scaled, wqkv[:, own], preferred_element_type=F32)
            chunks[c]["part"][:, :, :, own] = product.astype(BF16).reshape(4, 4, rpc * STEPS, half)
            for k in (1, 2, 3):
                if h == 0:
                    block, device = chunks[c]["part"].at[:, wrap(x, k), :, own], at_x(k)
                else:
                    block, device = chunks[c]["part"].at[wrap(y, k), :, :, own], at_y(k)
                out.append(remote(block, chunks[c]["ra"].at[h, k - 1], device))
        squares = embedded * embedded
        high = squares.astype(BF16)
        low = (squares - high.astype(F32)).astype(BF16)
        ones = jnp.ones((8, eall.shape[-1]), BF16)
        contract = (((1,), (1,)), ((), ()))
        total = lax.dot_general(ones, high, contract, preferred_element_type=F32)
        total = total + lax.dot_general(ones, low, contract, preferred_element_type=F32)
        chunks[c]["sq"][0] = total[:1]
        for k in (1, 2, 3):
            out.append(remote(chunks[c]["sq"].at[0], chunks[c]["rsq"].at[0, k - 1], at_x(k)))
        return out

    def send_2b(c, copies):
        for copy in copies:
            copy.wait_recv()
        chunks[c]["sq"][1] = (chunks[c]["sq"][0] + chunks[c]["rsq"][0, 0]) + (chunks[c]["rsq"][0, 1] + chunks[c]["rsq"][0, 2])
        out = []
        for h, own in ((0, chunks[c]["part"][:, x, :, pl.ds(0, half)]), (1, chunks[c]["part"][y, :, :, pl.ds(half, half)])):
            total = own.astype(F32)
            for k in range(3):
                total = total + chunks[c]["ra"][h, k].astype(F32)
            chunks[c]["sb"][h] = total.astype(BF16)
            for k in (1, 2, 3):
                if h == 0:
                    out.append(remote(chunks[c]["sb"].at[0, wrap(y, k)], chunks[c]["rb"].at[0, k - 1], at_y(k)))
                    out.append(remote(chunks[c]["sq"].at[1], chunks[c]["rsq"].at[1, k - 1], at_y(k)))
                else:
                    out.append(remote(chunks[c]["sb"].at[1, wrap(x, k)], chunks[c]["rb"].at[1, k - 1], at_x(k)))
        return out

    def rotary():
        entry = iota((ROWS * STEPS, 1), 0)
        length = jnp.zeros_like(entry)
        for r in range(ROWS):
            length = jnp.where(entry // STEPS == r, len_ref[r], length)
        angle = (length + entry % STEPS).astype(F32) * freq_ref[...]
        sine = jnp.sin(angle)
        turn[0] = jnp.cos(angle)
        turn[1] = jnp.where(iota(sine.shape, 1) < HD // 2, -sine, sine)

    def queries(c, copies):
        first, rpc = CHUNKS[c]
        tpd = rpc * STEPS
        tok = 16 * tpd
        for copy in copies:
            copy.wait_recv()
        squares = (chunks[c]["sq"][1] + chunks[c]["rsq"][1, 0]) + (chunks[c]["rsq"][1, 1] + chunks[c]["rsq"][1, 2])
        place = iota((tpd, tok), 1) == iota((tpd, tok), 0) + gy * tpd
        column = jnp.sum(jnp.where(place, squares, 0.0), axis=1, keepdims=True)
        inverse_rms = lax.rsqrt(column / D + EPS)
        pieces = []
        for h, own in ((0, chunks[c]["sb"][0, y]), (1, chunks[c]["sb"][1, x])):
            total = own.astype(F32)
            for k in range(3):
                total = total + chunks[c]["rb"][h, k].astype(F32)
            pieces.append(total)
        projected = jnp.concatenate(pieces, axis=1) * inverse_rms
        own = pl.ds(first * STEPS, tpd)
        cosine, sine = turn[0, own], turn[1, own]

        def rotate(g):
            field = projected[:, g * HD : (g + 1) * HD]
            return field * cosine + pltpu.roll(field, HD // 2, 1) * sine

        heads = [rotate(g) * HD ** (-0.5) for g in range(GROUP)]
        new_key = rotate(GROUP).astype(BF16)
        new_value = projected[:, (GROUP + 1) * HD :].astype(BF16)
        fresh = jnp.concatenate([new_key, new_value], axis=1)
        kvs[pl.ds(first * STEPS, tpd)] = fresh.astype(F32)
        rows = [
            jnp.concatenate([head[r * STEPS : (r + 1) * STEPS] for head in heads], axis=0)
            for r in range(rpc)
        ]
        return jnp.concatenate(rows, axis=0).astype(BF16), new_key, new_value

    nq = GROUP * STEPS

    def turn_keys(c):
        first, rpc = CHUNKS[c]
        for copy in load_kv[c]:
            copy.wait()

        @pl.loop(0, rpc * kbuf.shape[1] // TURN, unroll=2)
        def _(n):
            per_row = kbuf.shape[1] // TURN
            r = first + n // per_row
            where = pl.ds(pl.multiple_of(n % per_row * TURN, TURN), TURN)
            kturned[r, :, where] = kbuf[r, where].T

    def attention_scores(c, query, new_key):
        first, rpc = CHUNKS[c]
        fresh = lax.dot_general(
            query, new_key, (((1,), (1,)), ((), ())), preferred_element_type=F32
        )
        ask = iota(fresh.shape, 0)
        entry = iota(fresh.shape, 1)
        allowed = (entry // STEPS == ask // nq) & (entry % STEPS <= ask % STEPS)
        fresh = jnp.where(allowed, fresh, MASKED)

        def step(b, largest):
            start = pl.multiple_of(b * PBLK, PBLK)
            where = pl.ds(start, PBLK)
            place = iota((nq, PBLK), 1) + start
            larger = []
            for i in range(rpc):
                own = slice(i * nq, (i + 1) * nq)
                block = jnp.dot(
                    query[own], kturned[first + i, :, where], preferred_element_type=F32
                )
                block = jnp.where(place < len_ref[first + i], block, MASKED)
                scores[b, own] = block
                top = largest[i]
                for n in range(0, PBLK, HD):
                    top = jnp.maximum(top, block[:, n : n + HD])
                larger.append(top)
            return tuple(larger)

        least = jnp.full((nq, HD), MASKED, F32)
        largest = lax.fori_loop(0, scores.shape[0], step, (least,) * rpc, unroll=2)
        largest = jnp.concatenate(largest, axis=0)
        largest = jnp.maximum(
            jnp.max(largest, axis=1, keepdims=True), jnp.max(fresh, axis=1, keepdims=True)
        )
        return allowed, fresh, largest

    def attention_values(c, state, new_value):
        first, rpc = CHUNKS[c]
        allowed, fresh, largest = state
        fresh = jnp.where(allowed, jnp.exp(fresh - largest), 0.0)
        fresh_total = jnp.sum(fresh, axis=1, keepdims=True)
        fresh_value = jnp.dot(fresh.astype(BF16), new_value, preferred_element_type=F32)
        level = jnp.broadcast_to(largest, (rpc * nq, HD))

        def step(b, state):
            where = pl.ds(pl.multiple_of(b * PBLK, PBLK), PBLK)
            later = []
            for i in range(rpc):
                own = slice(i * nq, (i + 1) * nq)
                total, value = state[i]
                pieces = []
                for n in range(0, PBLK, HD):
                    piece = jnp.exp(scores[b, own, n : n + HD] - level[own])
                    total = total + piece
                    pieces.append(piece.astype(BF16))
                weights = jnp.concatenate(pieces, axis=1)
                value = value + jnp.dot(
                    weights, vbuf[first + i, where], preferred_element_type=F32
                )
                later.append((total, value))
            return tuple(later)

        nothing = jnp.zeros((nq, HD), F32)
        result = lax.fori_loop(
            0, scores.shape[0], step, ((nothing, nothing),) * rpc, unroll=2
        )
        total = jnp.concatenate([total for total, _ in result], axis=0)
        value = jnp.concatenate([value for _, value in result], axis=0)
        return jnp.sum(total, axis=1, keepdims=True) + fresh_total, value + fresh_value

    def send_4a(c, state):
        rpc = CHUNKS[c][1]
        total, value = state
        value = value / total
        columns = []
        for g in range(GROUP):
            columns.append(jnp.concatenate(
                [
                    value[r * nq + g * STEPS : r * nq + (g + 1) * STEPS]
                    for r in range(rpc)
                ],
                axis=0,
            ))
        chunks[c]["ag"][0, 0] = jnp.concatenate(columns, axis=1).astype(BF16)
        own = chunks[c]["ag"].at[0, 0]
        out = ([], [])
        for k in (1, 2, 3):
            out[0].append(remote(own, chunks[c]["ag"].at[0, k], at_x(k)))
            out[1].append(remote(own, chunks[c]["ag"].at[k, 0], at_y(k)))
        return out

    ahalf = wout.shape[0] // 2

    def send_4b(c, copies):
        along_x, along_y = copies
        out = []
        left, right = pl.ds(0, ahalf), pl.ds(ahalf, ahalf)
        others = pl.ds(1, 3)
        for copy in along_x:
            copy.wait_recv()
        for k in (1, 2, 3):
            out.append(remote(
                chunks[c]["ag"].at[0, others, :, left], chunks[c]["ag"].at[k, others, :, left], at_y(k)
            ))
        for copy in along_y:
            copy.wait_recv()
        for k in (1, 2, 3):
            out.append(remote(
                chunks[c]["ag"].at[others, 0, :, right], chunks[c]["ag"].at[others, k, :, right], at_x(k)
            ))
        return out

    def send_5a(c, copies):
        for copy in copies:
            copy.wait_recv()
        tpd = CHUNKS[c][1] * STEPS
        everyone = chunks[c]["ag"][...].reshape(16 * tpd, wout.shape[0])
        product = jnp.dot(everyone, wout[...], preferred_element_type=F32).astype(BF16)
        for ky in range(4):
            for kx in range(4):
                n = (ky * 4 + kx) * tpd
                place = wrap(x, 4 - kx)
                chunks[c]["part5"][wrap(y, 4 - ky), place // 2, place % 2] = product[n : n + tpd]
        return remote(chunks[c]["part5"].at[:, 1 - core], chunks[c]["r5a"], at_core())

    def send_5b(c, copy):
        copy.wait_recv()
        chunks[c]["s5"][...] = (chunks[c]["part5"][:, core].astype(F32) + chunks[c]["r5a"][...].astype(F32)).astype(BF16)
        return [remote(chunks[c]["s5"].at[wrap(z, k)], chunks[c]["r5b"].at[k - 1], at_z(k)) for k in (1, 2, 3)]

    def finish(c, copies):
        for copy in copies:
            copy.wait_recv()
        total = chunks[c]["s5"][z].astype(F32)
        for k in range(3):
            total = total + chunks[c]["r5b"][k].astype(F32)
        first, rpc = CHUNKS[c]
        size = 2 * rpc * STEPS
        fin[pl.ds(2 * first * STEPS, size)] = total.astype(BF16).reshape(size, total.shape[-1])

    for b in range(nblk):
        table_copies[b].wait()
        if b == nblk - 1:
            start_loads()
        gather(0, b)
    pl.semaphore_wait(barrier, len(partners))
    a1 = send_1a(0)
    for b in range(nblk // 2):
        gather(1, b)
    a1 = send_1b(0, a1)
    for b in range(nblk // 2, nblk):
        gather(1, b)
    b1 = send_1a(1)
    b1 = send_1b(1, b1)
    a1 = send_1c(0, a1)
    b1 = send_1c(1, b1)
    a1 = send_1d(0, a1)
    load_w.wait()
    for copy in a1:
        copy.wait_recv()
    p2 = [send_2a(0)]
    b1 = send_1d(1, b1)
    for copy in b1:
        copy.wait_recv()
    p2 += [send_2a(1), send_2a(2)]
    turn_keys(0)
    rotary()
    p2[0] = send_2b(0, p2[0])
    turn_keys(1)
    turn_keys(2)
    p2[1] = send_2b(1, p2[1])
    p4 = []
    query, new_key, new_value = queries(0, p2[0])
    state = attention_scores(0, query, new_key)
    p2[2] = send_2b(2, p2[2])
    p4.append(send_4a(0, attention_values(0, state, new_value)))
    for c in (1, 2):
        query, new_key, new_value = queries(c, p2[c])
        state = attention_scores(c, query, new_key)
        p4.append(send_4a(c, attention_values(c, state, new_value)))
    load_o.wait()
    p4[0] = send_4b(0, p4[0])
    p4[1] = send_4b(1, p4[1])
    p4[2] = send_4b(2, p4[2])
    p5 = [send_5a(0, p4[0])]
    p5.append(send_5a(1, p4[1]))
    p5[0] = send_5b(0, p5[0])
    p5.append(send_5a(2, p4[2]))
    p5[1] = send_5b(1, p5[1])
    p5[2] = send_5b(2, p5[2])
    for copy in sends:
        copy.wait_send()
    for c in range(len(CHUNKS)):
        finish(c, p5[c])


def order_outputs(fin, kvs, out_ref, kv_ref):
    size = ROWS * STEPS
    order = iota((size, size), 0)
    source = order % ROWS * STEPS + order // ROWS
    perm = jnp.where(iota((size, size), 1) == source, 1.0, 0.0).astype(BF16)
    fresh = jnp.dot(perm, kvs[...].astype(BF16), preferred_element_type=F32).astype(BF16)
    kv_ref[0] = fresh[:, :HD]
    kv_ref[1] = fresh[:, HD:]

    size = 2 * ROWS * STEPS
    order = iota((size, size), 0)
    step, side, row = order // (2 * ROWS), order // ROWS % 2, order % ROWS
    source = order
    for first, rpc in CHUNKS:
        inside = (row >= first) & (row < first + rpc)
        place = 2 * first * STEPS + side * rpc * STEPS + (row - first) * STEPS + step
        source = jnp.where(inside, place, source)
    perm = jnp.where(iota((size, size), 1) == source, 1.0, 0.0).astype(BF16)
    out_ref[...] = jnp.dot(perm, fin[...], preferred_element_type=F32).astype(BF16)


COPIES = NGR * (1 + 3 + 3 + 4) + len(CHUNKS) * (9 + 9 + 6 + 6 + 1 + 3)


def chunk_scratch(rows, cols, width, out_cols):
    tpd = rows * STEPS
    tok = 16 * tpd
    half = cols // 2
    return {
        "part": pltpu.VMEM((4, 4, tpd, cols), BF16),
        "ra": pltpu.VMEM((2, 3, 4, tpd, half), BF16),
        "sb": pltpu.VMEM((2, 4, tpd, half), BF16),
        "rb": pltpu.VMEM((2, 3, tpd, half), BF16),
        "sq": pltpu.VMEM((2, 1, tok), F32),
        "rsq": pltpu.VMEM((2, 3, 1, tok), F32),
        "ag": pltpu.VMEM((4, 4, tpd, width), BF16),
        "part5": pltpu.VMEM((4, 2, 2, tpd, out_cols), BF16),
        "r5a": pltpu.VMEM((4, 2, tpd, out_cols), BF16),
        "s5": pltpu.VMEM((4, 2, tpd, out_cols), BF16),
        "r5b": pltpu.VMEM((3, 2, tpd, out_cols), BF16),
    }


def body(
    token_ids, cache_lengths, embed_table, norm_gain, qkv_weight, key_cache, value_cache, out_weight
):
    vocab, feats = embed_table.shape
    cols = qkv_weight.shape[1]
    width, out_cols = out_weight.shape
    frequency = THETA ** (-np.arange(HD // 2, dtype=np.float64) * (2.0 / HD))
    frequency = np.concatenate([frequency, frequency]).astype(np.float32)[None, :]
    vmem = pl.BlockSpec(memory_space=pltpu.VMEM)
    hbm = pl.BlockSpec(memory_space=pl.ANY)
    smem = pl.BlockSpec(memory_space=pltpu.SMEM)
    dma = pltpu.SemaphoreType.DMA
    fin, kvs = pl.pallas_call(
        kernel,
        out_shape=(
            jax.ShapeDtypeStruct((2 * ROWS * STEPS, out_cols), BF16),
            jax.ShapeDtypeStruct((ROWS * STEPS, 2 * HD), F32),
        ),
        in_specs=[smem] + [hbm] * 8,
        out_specs=(vmem, vmem),
        scratch_shapes=[
            pltpu.VMEM(token_ids.shape, jnp.int32),
            pltpu.VMEM(norm_gain.shape, BF16),
            pltpu.VMEM(frequency.shape, F32),
            pltpu.VMEM((vocab // TBLK, TBLK, feats), BF16),
            pltpu.VMEM(qkv_weight.shape, BF16),
            pltpu.VMEM(out_weight.shape, BF16),
            pltpu.VMEM(key_cache.shape, BF16),
            pltpu.VMEM((key_cache.shape[0], HD, key_cache.shape[1]), BF16),
            pltpu.VMEM(value_cache.shape, BF16),
            pltpu.VMEM((NGR, GTOK, feats), F32),
            pltpu.VMEM((NGR, 4, 2, GSL, feats), BF16),
            pltpu.VMEM((NGR, 4, GSL, feats), BF16),
            pltpu.VMEM((NGR, 4, GSL, feats), BF16),
            pltpu.VMEM((NGR, 3, GSL, feats), BF16),
            pltpu.VMEM((NGR, 4, 2, GSL, feats), BF16),
            pltpu.VMEM((key_cache.shape[1] // PBLK, 2 * GROUP * STEPS, PBLK), F32),
            pltpu.VMEM((2, ROWS * STEPS, HD), F32),
            [chunk_scratch(rows, cols, width, out_cols) for _, rows in CHUNKS],
            dma((3,)),
            dma((2 + 2 * len(CHUNKS),)),
            dma((vocab // TBLK,)),
            dma((COPIES,)),
            dma((COPIES,)),
        ],
        compiler_params=pltpu.CompilerParams(
            collective_id=0, has_side_effects=True, vmem_limit_bytes=56 << 20
        ),
        cost_estimate=pl.CostEstimate(
            flops=8 * 10**9, bytes_accessed=30 * 10**6, transcendentals=2 * 10**6
        ),
        name="decode_block",
    )(
        cache_lengths, token_ids, norm_gain, jnp.asarray(frequency), embed_table,
        qkv_weight, key_cache, value_cache, out_weight,
    )
    out, kv = pl.pallas_call(
        order_outputs,
        out_shape=(
            jax.ShapeDtypeStruct((2 * ROWS * STEPS, out_cols), BF16),
            jax.ShapeDtypeStruct((2, ROWS * STEPS, HD), BF16),
        ),
        in_specs=[vmem, vmem],
        out_specs=(vmem, vmem),
        name="order_outputs",
    )(fin, kvs)
    return (
        out.reshape(STEPS, 2 * ROWS, out_cols),
        kv.reshape(2, STEPS, ROWS, HD),
    )


def solution(mesh):
    in_specs = (
        P(),
        P("gy"),
        P("gx", "gy"),
        P("gy"),
        P("gy", "gx"),
        P("gy", None, "gx"),
        P("gy", None, "gx"),
        P("gx", "gy"),
    )
    out_specs = (P(None, "gx", "gy"), P(None, None, "gy", "gx"))
    return jax.shard_map(body, mesh=mesh, in_specs=in_specs, out_specs=out_specs, check_vma=False)
```

```python
import functools
import math

import jax
import jax.numpy as jnp
import numpy as np
from jax import lax
from jax.experimental import pallas as pl
from jax.experimental.pallas import tpu as pltpu
from jax.sharding import PartitionSpec as P

D = 8192
HD = 128
GROUP = 8
STEPS = 8
THETA = 500000.0
EPS = 1e-05
MASKED = -1e30
MESH = pl.DeviceIdType.MESH

ROWS = 4
CHUNKS = ((0, 2), (2, 1), (3, 1))
NGR = 2
PARTS = ((0,), (1, 2))
GTOK = 16 * 2 * STEPS
GSL = GTOK // 8
TBLK = 2048
PBLK = 4096
TURN = 1024
F32 = jnp.float32
BF16 = jnp.bfloat16


def iota(shape, dim):
    return lax.broadcasted_iota(jnp.int32, shape, dim)


def kernel(
    len_ref, ids_hbm, gain_hbm, freq_hbm, table_hbm, wqkv_hbm, key_hbm, val_hbm, wout_hbm,
    fin, kvs,
    ids_ref, gain_ref, freq_ref, table, wqkv, wout, kbuf, kturned, vbuf, acc,
    picks, r1a, s1, r1b, eall, scores, turn, chunks,
    small_sem, local_sem, table_sem, send_sem, recv_sem,
):
    gx = lax.axis_index("gx")
    gy = lax.axis_index("gy")
    z, core = gx // 2, gx % 2
    y, x = gy // 4, gy % 4

    def wrap(a, k):
        return (a + k) % 4

    def at_core():
        return (z * 2 + 1 - core, gy)

    def at_z(k):
        return (wrap(z, k) * 2 + core, gy)

    def at_y(k):
        return (gx, wrap(y, k) * 4 + x)

    def at_x(k):
        return (gx, y * 4 + wrap(x, k))

    counter = [0]
    sends = []

    def remote(src, dst, device):
        n = counter[0]
        counter[0] += 1
        copy = pltpu.make_async_remote_copy(
            src_ref=src, dst_ref=dst, send_sem=send_sem.at[n], recv_sem=recv_sem.at[n],
            device_id=device, device_id_type=MESH,
        )
        copy.start()
        sends.append(copy)
        return copy

    small = [
        pltpu.make_async_copy(hbm, ref, small_sem.at[n])
        for n, (hbm, ref) in enumerate(
            ((ids_hbm, ids_ref), (gain_hbm, gain_ref), (freq_hbm, freq_ref))
        )
    ]
    for copy in small:
        copy.start()
    nblk = table.shape[0]
    table_copies = []
    for b in range(nblk):
        copy = pltpu.make_async_copy(
            table_hbm.at[pl.ds(b * TBLK, TBLK)], table.at[b], table_sem.at[b]
        )
        copy.start()
        table_copies.append(copy)
    load_w = pltpu.make_async_copy(wqkv_hbm, wqkv, local_sem.at[0])
    load_o = pltpu.make_async_copy(wout_hbm, wout, local_sem.at[1])
    load_kv = []
    for first, rpc in CHUNKS:
        rows = pl.ds(first, rpc)
        c = len(load_kv)
        load_kv.append((
            pltpu.make_async_copy(key_hbm.at[rows], kbuf.at[rows], local_sem.at[2 + 2 * c]),
            pltpu.make_async_copy(val_hbm.at[rows], vbuf.at[rows], local_sem.at[3 + 2 * c]),
        ))

    def start_loads():
        load_w.start()
        for pair in load_kv:
            for copy in pair:
                copy.start()
        load_o.start()

    barrier = pltpu.get_barrier_semaphore()
    partners = [at_core()]
    for k in (1, 2, 3):
        partners += [at_z(k), at_y(k), at_x(k)]
    for device in partners:
        pl.semaphore_signal(barrier, inc=1, device_id=device, device_id_type=MESH)

    for copy in small:
        copy.wait()
    ids = ids_ref[...]
    id_high = (ids >> 8).astype(F32).astype(BF16)
    id_low = (ids & 255).astype(F32).astype(BF16)

    def local_ids(g):
        first, rpc = CHUNKS[PARTS[g][0]]
        token = iota((GTOK, 64), 0)
        place = token % (16 * rpc * STEPS)
        row = place // (rpc * STEPS) * ROWS + first
        row = row + token // (16 * rpc * STEPS) + place // STEPS % rpc
        chosen = jnp.where(iota((GTOK, 64), 1) == row, 1.0, 0.0).astype(BF16)
        contract = (((1,), (1,)), ((), ()))
        high = lax.dot_general(chosen, id_high, contract, preferred_element_type=F32)
        low = lax.dot_general(chosen, id_low, contract, preferred_element_type=F32)
        both = high * 256.0 + low
        mine = iota((GTOK, STEPS), 1) == iota((GTOK, STEPS), 0) % STEPS
        column = jnp.sum(jnp.where(mine, both, 0.0), axis=1, keepdims=True)
        return column.astype(jnp.int32) - gx * (nblk * TBLK)

    local = [local_ids(g) for g in range(NGR)]

    def gather(c, b):
        hot = jnp.where(iota((GTOK, TBLK), 1) == local[c] - b * TBLK, 1.0, 0.0).astype(BF16)
        term = jnp.dot(hot, table[b], preferred_element_type=F32)
        if b == 0:
            acc[c] = term
        elif b < nblk - 1:
            acc[c] += term
        else:
            picks[c] = (acc[c] + term).astype(BF16).reshape(picks.shape[1:])

    def send_1a(c):
        return remote(picks.at[c, :, 1 - core], r1a.at[c], at_core())

    def send_1b(c, copy):
        copy.wait_recv()
        s1[c] = picks[c, :, core] + r1a[c]
        return [remote(s1.at[c, wrap(z, k)], r1b.at[c, k - 1], at_z(k)) for k in (1, 2, 3)]

    def send_1c(c, copies):
        for copy in copies:
            copy.wait_recv()
        eall[c, z, core] = (s1[c, z] + r1b[c, 0]) + (r1b[c, 1] + r1b[c, 2])
        mine = eall.at[c, z, core]
        return (
            [remote(mine, mine, at_z(k)) for k in (1, 2, 3)],
            [remote(mine, mine, at_core())],
        )

    def send_1d(c, copies):
        across, over = copies
        for k, copy in zip((1, 2, 3), across):
            copy.wait_recv()
            block = eall.at[c, wrap(z, 4 - k), core]
            over.append(remote(block, block, at_core()))
        return over

    half = wqkv.shape[1] // 2

    def send_2a(c):
        rpc = CHUNKS[c][1]
        tok = 16 * rpc * STEPS
        g = 0 if c in PARTS[0] else 1
        size = 4 // len(PARTS[g])
        embedded = eall[g, pl.ds(PARTS[g].index(c) * size, size)]
        embedded = embedded.reshape(tok, eall.shape[-1]).astype(F32)
        scaled = (embedded * gain_ref[...].astype(F32)[None, :]).astype(BF16)
        out = []
        for h in range(2):
            own = pl.ds(h * half, half)
            product = jnp.dot(scaled, wqkv[:, own], preferred_element_type=F32)
            chunks[c]["part"][:, :, :, own] = product.astype(BF16).reshape(4, 4, rpc * STEPS, half)
            for k in (1, 2, 3):
                if h == 0:
                    block, device = chunks[c]["part"].at[:, wrap(x, k), :, own], at_x(k)
                else:
                    block, device = chunks[c]["part"].at[wrap(y, k), :, :, own], at_y(k)
                out.append(remote(block, chunks[c]["ra"].at[h, k - 1], device))
        return out

    def send_squares(c):
        g = 0 if c in PARTS[0] else 1
        size = 4 // len(PARTS[g])
        embedded = eall[g, pl.ds(PARTS[g].index(c) * size, size)]
        embedded = embedded.reshape(16 * CHUNKS[c][1] * STEPS, eall.shape[-1]).astype(F32)
        out = []
        squares = embedded * embedded
        high = squares.astype(BF16)
        low = (squares - high.astype(F32)).astype(BF16)
        ones = jnp.ones((8, eall.shape[-1]), BF16)
        contract = (((1,), (1,)), ((), ()))
        total = lax.dot_general(ones, high, contract, preferred_element_type=F32)
        total = total + lax.dot_general(ones, low, contract, preferred_element_type=F32)
        chunks[c]["sq"][0] = total[:1]
        for k in (1, 2, 3):
            out.append(remote(chunks[c]["sq"].at[0], chunks[c]["rsq"].at[0, k - 1], at_x(k)))
        return out

    def send_2b(c, copies):
        for copy in copies:
            copy.wait_recv()
        chunks[c]["sq"][1] = (chunks[c]["sq"][0] + chunks[c]["rsq"][0, 0]) + (chunks[c]["rsq"][0, 1] + chunks[c]["rsq"][0, 2])
        out = []
        for h, own in ((0, chunks[c]["part"][:, x, :, pl.ds(0, half)]), (1, chunks[c]["part"][y, :, :, pl.ds(half, half)])):
            total = own.astype(F32)
            for k in range(3):
                total = total + chunks[c]["ra"][h, k].astype(F32)
            chunks[c]["sb"][h] = total.astype(BF16)
            for k in (1, 2, 3):
                if h == 0:
                    out.append(remote(chunks[c]["sb"].at[0, wrap(y, k)], chunks[c]["rb"].at[0, k - 1], at_y(k)))
                    out.append(remote(chunks[c]["sq"].at[1], chunks[c]["rsq"].at[1, k - 1], at_y(k)))
                else:
                    out.append(remote(chunks[c]["sb"].at[1, wrap(x, k)], chunks[c]["rb"].at[1, k - 1], at_x(k)))
        return out

    def rotary():
        entry = iota((ROWS * STEPS, 1), 0)
        length = jnp.zeros_like(entry)
        for r in range(ROWS):
            length = jnp.where(entry // STEPS == r, len_ref[r], length)
        angle = (length + entry % STEPS).astype(F32) * freq_ref[...]
        sine = jnp.sin(angle)
        turn[0] = jnp.cos(angle)
        turn[1] = jnp.where(iota(sine.shape, 1) < HD // 2, -sine, sine)

    def queries(c, copies):
        first, rpc = CHUNKS[c]
        tpd = rpc * STEPS
        tok = 16 * tpd
        for copy in copies:
            copy.wait_recv()
        squares = (chunks[c]["sq"][1] + chunks[c]["rsq"][1, 0]) + (chunks[c]["rsq"][1, 1] + chunks[c]["rsq"][1, 2])
        place = iota((tpd, tok), 1) == iota((tpd, tok), 0) + gy * tpd
        column = jnp.sum(jnp.where(place, squares, 0.0), axis=1, keepdims=True)
        inverse_rms = lax.rsqrt(column / D + EPS)
        pieces = []
        for h, own in ((0, chunks[c]["sb"][0, y]), (1, chunks[c]["sb"][1, x])):
            total = own.astype(F32)
            for k in range(3):
                total = total + chunks[c]["rb"][h, k].astype(F32)
            pieces.append(total)
        projected = jnp.concatenate(pieces, axis=1) * inverse_rms
        own = pl.ds(first * STEPS, tpd)
        cosine, sine = turn[0, own], turn[1, own]

        def rotate(g):
            field = projected[:, g * HD : (g + 1) * HD]
            return field * cosine + pltpu.roll(field, HD // 2, 1) * sine

        heads = [rotate(g) * HD ** (-0.5) for g in range(GROUP)]
        new_key = rotate(GROUP).astype(BF16)
        new_value = projected[:, (GROUP + 1) * HD :].astype(BF16)
        fresh = jnp.concatenate([new_key, new_value], axis=1)
        kvs[pl.ds(first * STEPS, tpd)] = fresh.astype(F32)
        rows = [
            jnp.concatenate([head[r * STEPS : (r + 1) * STEPS] for head in heads], axis=0)
            for r in range(rpc)
        ]
        return jnp.concatenate(rows, axis=0).astype(BF16), new_key, new_value

    nq = GROUP * STEPS

    def turn_keys(c):
        first, rpc = CHUNKS[c]
        for copy in load_kv[c]:
            copy.wait()

        @pl.loop(0, rpc * kbuf.shape[1] // TURN, unroll=2)
        def _(n):
            per_row = kbuf.shape[1] // TURN
            r = first + n // per_row
            where = pl.ds(pl.multiple_of(n % per_row * TURN, TURN), TURN)
            kturned[r, :, where] = kbuf[r, where].T

    def attention_scores(c, query, new_key):
        first, rpc = CHUNKS[c]
        fresh = lax.dot_general(
            query, new_key, (((1,), (1,)), ((), ())), preferred_element_type=F32
        )
        ask = iota(fresh.shape, 0)
        entry = iota(fresh.shape, 1)
        allowed = (entry // STEPS == ask // nq) & (entry % STEPS <= ask % STEPS)
        fresh = jnp.where(allowed, fresh, MASKED)

        def step(b, largest):
            start = pl.multiple_of(b * PBLK, PBLK)
            where = pl.ds(start, PBLK)
            place = iota((nq, PBLK), 1) + start
            larger = []
            for i in range(rpc):
                own = slice(i * nq, (i + 1) * nq)
                block = jnp.dot(
                    query[own], kturned[first + i, :, where], preferred_element_type=F32
                )
                block = jnp.where(place < len_ref[first + i], block, MASKED)
                scores[b, own] = block
                top = largest[i]
                for n in range(0, PBLK, HD):
                    top = jnp.maximum(top, block[:, n : n + HD])
                larger.append(top)
            return tuple(larger)

        least = jnp.full((nq, HD), MASKED, F32)
        largest = lax.fori_loop(0, scores.shape[0], step, (least,) * rpc, unroll=2)
        largest = jnp.concatenate(largest, axis=0)
        largest = jnp.maximum(
            jnp.max(largest, axis=1, keepdims=True), jnp.max(fresh, axis=1, keepdims=True)
        )
        return allowed, fresh, largest

    def attention_values(c, state, new_value):
        first, rpc = CHUNKS[c]
        allowed, fresh, largest = state
        fresh = jnp.where(allowed, jnp.exp(fresh - largest), 0.0)
        fresh_total = jnp.sum(fresh, axis=1, keepdims=True)
        fresh_value = jnp.dot(fresh.astype(BF16), new_value, preferred_element_type=F32)
        level = jnp.broadcast_to(largest, (rpc * nq, HD))

        def step(b, state):
            where = pl.ds(pl.multiple_of(b * PBLK, PBLK), PBLK)
            later = []
            for i in range(rpc):
                own = slice(i * nq, (i + 1) * nq)
                total, value = state[i]
                pieces = []
                for n in range(0, PBLK, HD):
                    piece = jnp.exp(scores[b, own, n : n + HD] - level[own])
                    total = total + piece
                    pieces.append(piece.astype(BF16))
                weights = jnp.concatenate(pieces, axis=1)
                value = value + jnp.dot(
                    weights, vbuf[first + i, where], preferred_element_type=F32
                )
                later.append((total, value))
            return tuple(later)

        nothing = jnp.zeros((nq, HD), F32)
        result = lax.fori_loop(
            0, scores.shape[0], step, ((nothing, nothing),) * rpc, unroll=2
        )
        total = jnp.concatenate([total for total, _ in result], axis=0)
        value = jnp.concatenate([value for _, value in result], axis=0)
        return jnp.sum(total, axis=1, keepdims=True) + fresh_total, value + fresh_value

    def send_4a(c, state):
        rpc = CHUNKS[c][1]
        total, value = state
        value = value / total
        columns = []
        for g in range(GROUP):
            columns.append(jnp.concatenate(
                [
                    value[r * nq + g * STEPS : r * nq + (g + 1) * STEPS]
                    for r in range(rpc)
                ],
                axis=0,
            ))
        chunks[c]["ag"][0, 0] = jnp.concatenate(columns, axis=1).astype(BF16)
        own = chunks[c]["ag"].at[0, 0]
        out = ([], [])
        for k in (1, 2, 3):
            out[0].append(remote(own, chunks[c]["ag"].at[0, k], at_x(k)))
            out[1].append(remote(own, chunks[c]["ag"].at[k, 0], at_y(k)))
        return out

    ahalf = wout.shape[0] // 2

    def send_4b(c, copies):
        along_x, along_y = copies
        out = []
        left, right = pl.ds(0, ahalf), pl.ds(ahalf, ahalf)
        others = pl.ds(1, 3)
        for copy in along_x:
            copy.wait_recv()
        for k in (1, 2, 3):
            out.append(remote(
                chunks[c]["ag"].at[0, others, :, left], chunks[c]["ag"].at[k, others, :, left], at_y(k)
            ))
        for copy in along_y:
            copy.wait_recv()
        for k in (1, 2, 3):
            out.append(remote(
                chunks[c]["ag"].at[others, 0, :, right], chunks[c]["ag"].at[others, k, :, right], at_x(k)
            ))
        return out

    def send_5a(c, copies):
        for copy in copies:
            copy.wait_recv()
        tpd = CHUNKS[c][1] * STEPS
        everyone = chunks[c]["ag"][...].reshape(16 * tpd, wout.shape[0])
        product = jnp.dot(everyone, wout[...], preferred_element_type=F32).astype(BF16)
        for ky in range(4):
            for kx in range(4):
                n = (ky * 4 + kx) * tpd
                place = wrap(x, 4 - kx)
                chunks[c]["part5"][wrap(y, 4 - ky), place // 2, place % 2] = product[n : n + tpd]
        return remote(chunks[c]["part5"].at[:, 1 - core], chunks[c]["r5a"], at_core())

    def send_5b(c, copy):
        copy.wait_recv()
        chunks[c]["s5"][...] = (chunks[c]["part5"][:, core].astype(F32) + chunks[c]["r5a"][...].astype(F32)).astype(BF16)
        return [remote(chunks[c]["s5"].at[wrap(z, k)], chunks[c]["r5b"].at[k - 1], at_z(k)) for k in (1, 2, 3)]

    def finish(c, copies):
        for copy in copies:
            copy.wait_recv()
        total = chunks[c]["s5"][z].astype(F32)
        for k in range(3):
            total = total + chunks[c]["r5b"][k].astype(F32)
        first, rpc = CHUNKS[c]
        size = 2 * rpc * STEPS
        fin[pl.ds(2 * first * STEPS, size)] = total.astype(BF16).reshape(size, total.shape[-1])

    for b in range(nblk):
        table_copies[b].wait()
        if b == nblk - 1:
            start_loads()
        gather(0, b)
    pl.semaphore_wait(barrier, len(partners))
    a1 = send_1a(0)
    for b in range(nblk // 2):
        gather(1, b)
    a1 = send_1b(0, a1)
    for b in range(nblk // 2, nblk):
        gather(1, b)
    b1 = send_1a(1)
    b1 = send_1b(1, b1)
    a1 = send_1c(0, a1)
    b1 = send_1c(1, b1)
    a1 = send_1d(0, a1)
    load_w.wait()
    for copy in a1:
        copy.wait_recv()
    p2 = [send_2a(0)]
    p2[0] += send_squares(0)
    b1 = send_1d(1, b1)
    for copy in b1:
        copy.wait_recv()
    p2 += [send_2a(1), send_2a(2)]
    p2[1] += send_squares(1)
    p2[2] += send_squares(2)
    turn_keys(0)
    rotary()
    p2[0] = send_2b(0, p2[0])
    turn_keys(1)
    turn_keys(2)
    p2[1] = send_2b(1, p2[1])
    p4 = []
    query, new_key, new_value = queries(0, p2[0])
    state = attention_scores(0, query, new_key)
    p2[2] = send_2b(2, p2[2])
    p4.append(send_4a(0, attention_values(0, state, new_value)))
    for c in (1, 2):
        query, new_key, new_value = queries(c, p2[c])
        state = attention_scores(c, query, new_key)
        p4.append(send_4a(c, attention_values(c, state, new_value)))
    load_o.wait()
    p4[0] = send_4b(0, p4[0])
    p4[1] = send_4b(1, p4[1])
    p4[2] = send_4b(2, p4[2])
    p5 = [send_5a(0, p4[0])]
    p5.append(send_5a(1, p4[1]))
    p5[0] = send_5b(0, p5[0])
    p5.append(send_5a(2, p4[2]))
    p5[1] = send_5b(1, p5[1])
    p5[2] = send_5b(2, p5[2])
    for copy in sends:
        copy.wait_send()
    for c in range(len(CHUNKS)):
        finish(c, p5[c])


def order_outputs(fin, kvs, out_ref, kv_ref):
    size = ROWS * STEPS
    order = iota((size, size), 0)
    source = order % ROWS * STEPS + order // ROWS
    perm = jnp.where(iota((size, size), 1) == source, 1.0, 0.0).astype(BF16)
    fresh = jnp.dot(perm, kvs[...].astype(BF16), preferred_element_type=F32).astype(BF16)
    kv_ref[0] = fresh[:, :HD]
    kv_ref[1] = fresh[:, HD:]

    size = 2 * ROWS * STEPS
    order = iota((size, size), 0)
    step, side, row = order // (2 * ROWS), order // ROWS % 2, order % ROWS
    source = order
    for first, rpc in CHUNKS:
        inside = (row >= first) & (row < first + rpc)
        place = 2 * first * STEPS + side * rpc * STEPS + (row - first) * STEPS + step
        source = jnp.where(inside, place, source)
    perm = jnp.where(iota((size, size), 1) == source, 1.0, 0.0).astype(BF16)
    out_ref[...] = jnp.dot(perm, fin[...], preferred_element_type=F32).astype(BF16)


COPIES = NGR * (1 + 3 + 3 + 4) + len(CHUNKS) * (9 + 9 + 6 + 6 + 1 + 3)


def chunk_scratch(rows, cols, width, out_cols):
    tpd = rows * STEPS
    tok = 16 * tpd
    half = cols // 2
    return {
        "part": pltpu.VMEM((4, 4, tpd, cols), BF16),
        "ra": pltpu.VMEM((2, 3, 4, tpd, half), BF16),
        "sb": pltpu.VMEM((2, 4, tpd, half), BF16),
        "rb": pltpu.VMEM((2, 3, tpd, half), BF16),
        "sq": pltpu.VMEM((2, 1, tok), F32),
        "rsq": pltpu.VMEM((2, 3, 1, tok), F32),
        "ag": pltpu.VMEM((4, 4, tpd, width), BF16),
        "part5": pltpu.VMEM((4, 2, 2, tpd, out_cols), BF16),
        "r5a": pltpu.VMEM((4, 2, tpd, out_cols), BF16),
        "s5": pltpu.VMEM((4, 2, tpd, out_cols), BF16),
        "r5b": pltpu.VMEM((3, 2, tpd, out_cols), BF16),
    }


def body(
    token_ids, cache_lengths, embed_table, norm_gain, qkv_weight, key_cache, value_cache, out_weight
):
    vocab, feats = embed_table.shape
    cols = qkv_weight.shape[1]
    width, out_cols = out_weight.shape
    frequency = THETA ** (-np.arange(HD // 2, dtype=np.float64) * (2.0 / HD))
    frequency = np.concatenate([frequency, frequency]).astype(np.float32)[None, :]
    vmem = pl.BlockSpec(memory_space=pltpu.VMEM)
    hbm = pl.BlockSpec(memory_space=pl.ANY)
    smem = pl.BlockSpec(memory_space=pltpu.SMEM)
    dma = pltpu.SemaphoreType.DMA
    fin, kvs = pl.pallas_call(
        kernel,
        out_shape=(
            jax.ShapeDtypeStruct((2 * ROWS * STEPS, out_cols), BF16),
            jax.ShapeDtypeStruct((ROWS * STEPS, 2 * HD), F32),
        ),
        in_specs=[smem] + [hbm] * 8,
        out_specs=(vmem, vmem),
        scratch_shapes=[
            pltpu.VMEM(token_ids.shape, jnp.int32),
            pltpu.VMEM(norm_gain.shape, BF16),
            pltpu.VMEM(frequency.shape, F32),
            pltpu.VMEM((vocab // TBLK, TBLK, feats), BF16),
            pltpu.VMEM(qkv_weight.shape, BF16),
            pltpu.VMEM(out_weight.shape, BF16),
            pltpu.VMEM(key_cache.shape, BF16),
            pltpu.VMEM((key_cache.shape[0], HD, key_cache.shape[1]), BF16),
            pltpu.VMEM(value_cache.shape, BF16),
            pltpu.VMEM((NGR, GTOK, feats), F32),
            pltpu.VMEM((NGR, 4, 2, GSL, feats), BF16),
            pltpu.VMEM((NGR, 4, GSL, feats), BF16),
            pltpu.VMEM((NGR, 4, GSL, feats), BF16),
            pltpu.VMEM((NGR, 3, GSL, feats), BF16),
            pltpu.VMEM((NGR, 4, 2, GSL, feats), BF16),
            pltpu.VMEM((key_cache.shape[1] // PBLK, 2 * GROUP * STEPS, PBLK), F32),
            pltpu.VMEM((2, ROWS * STEPS, HD), F32),
            [chunk_scratch(rows, cols, width, out_cols) for _, rows in CHUNKS],
            dma((3,)),
            dma((2 + 2 * len(CHUNKS),)),
            dma((vocab // TBLK,)),
            dma((COPIES,)),
            dma((COPIES,)),
        ],
        compiler_params=pltpu.CompilerParams(
            collective_id=0, has_side_effects=True, vmem_limit_bytes=56 << 20
        ),
        cost_estimate=pl.CostEstimate(
            flops=8 * 10**9, bytes_accessed=30 * 10**6, transcendentals=2 * 10**6
        ),
        name="decode_block",
    )(
        cache_lengths, token_ids, norm_gain, jnp.asarray(frequency), embed_table,
        qkv_weight, key_cache, value_cache, out_weight,
    )
    out, kv = pl.pallas_call(
        order_outputs,
        out_shape=(
            jax.ShapeDtypeStruct((2 * ROWS * STEPS, out_cols), BF16),
            jax.ShapeDtypeStruct((2, ROWS * STEPS, HD), BF16),
        ),
        in_specs=[vmem, vmem],
        out_specs=(vmem, vmem),
        name="order_outputs",
    )(fin, kvs)
    return (
        out.reshape(STEPS, 2 * ROWS, out_cols),
        kv.reshape(2, STEPS, ROWS, HD),
    )


def solution(mesh):
    in_specs = (
        P(),
        P("gy"),
        P("gx", "gy"),
        P("gy"),
        P("gy", "gx"),
        P("gy", None, "gx"),
        P("gy", None, "gx"),
        P("gx", "gy"),
    )
    out_specs = (P(None, "gx", "gy"), P(None, None, "gy", "gx"))
    return jax.shard_map(body, mesh=mesh, in_specs=in_specs, out_specs=out_specs, check_vma=False)
```
